1024 devices in a mesh: island: 16 (over y, core), ep: 16 (over z), tp: 4 (over x).
Axes of the slice: x: 4, y: 8, z: 16, core: 2. Of those that a mesh axis runs over, the one named last changes fastest.
Arguments:
- tokens: bfloat16 [32768, 2048], P(('island', 'ep')), may hold values from -6 to 6
- cotangent: bfloat16 [32768, 2048], P(('island', 'ep')), may hold values from -6 to 6
- expert_ids: int32 [32768, 1], P(('island', 'ep')), may hold values from 0 to 15; in each aligned block of 128 rows (0 to 127, 128 to 255, ...) at most 10 rows name the same one
- gate_probs: float32 [32768, 1], P(('island', 'ep')), may hold values from 0.1 to 1
- w_gate: bfloat16 [16, 2048, 768], P('ep', None, 'tp'), may hold values from -0.125 to 0.125
- w_up: bfloat16 [16, 2048, 768], P('ep', None, 'tp'), may hold values from -0.125 to 0.125
- w_down: bfloat16 [16, 768, 2048], P('ep', 'tp'), may hold values from -0.21875 to 0.21875
Outputs:
- token_grad: bfloat16 [32768, 2048], P(('island', 'ep'), 'tp')
- prob_grad: float32 [32768, 1], P(('island', 'ep'))
- grad_gate: float32 [16, 2048, 768], P('ep', 'island', 'tp')
- grad_up: float32 [16, 2048, 768], P('ep', 'island', 'tp')
- grad_down: float32 [16, 768, 2048], P('ep', 'tp', 'island')
The draws below stay inside these ranges and needn't reach their ends.
Inputs may be any that keep to these rules, and one draw needn't show every extreme that they name: `expert_ids`: each row names one expert; in each aligned block of 128 rows (one index of island and ep) no expert is named by more than 10 rows, a bound that some block reaches.
All inputs are finite; a program needn't handle non-finite values.
Results may differ from the reference program's by a relative error of at most 0.025.
Values may be sent and summed in bfloat16 or wider, within the bound.
A program may use at most 32 MiB of HBM per device.

```python
import math
import jax
import jax.numpy as jnp
import numpy as np
from jax import lax

D = 2048
FF = 768
TOP = 1
TOK = 128
EXPERTS = 16
CAP = 10
TOKENS = 32768
N_TP = 4


def block_scale(own_key, extent, shards, low, high):
    level, own = 1.0, jax.random.fold_in(own_key, 6)
    for position, blocks in shards:
        draws = jnp.exp(jax.random.uniform(jax.random.fold_in(own, position), (blocks,), jnp.float32, low / len(shards), high / len(shards)))
        level = level * jnp.repeat(draws, extent[position] // blocks).reshape([-1 if axis == position else 1 for axis in range(len(extent))])
    return level


def routed_block(key, own, number, rows, amount, top, bound, lean):
    sequence = jax.random.permutation(key, amount)
    packed, usual = shares(amount, rows * top, bound, lean, True), shares(amount, rows * top, bound, lean, False)
    places = jnp.arange(amount)

    def named(sizes, rotation):
        used = int((sizes > 0).sum())
        fixed = max(1, used // 4)
        shifted = fixed + (places - fixed + rotation * (used - fixed)) % max(1, amount - fixed)
        return jnp.zeros((amount,), jnp.int32).at[sequence[jnp.where(places < fixed, places, shifted)]].set(jnp.asarray(sizes, jnp.int32))

    sizes = jnp.where(number % 4 == 0, named(packed, number // 4), named(usual, number - number // 4 - 1))
    mixed = jax.random.permutation(jax.random.fold_in(own, 3), amount)
    giver, taker = mixed[0:amount // 2 * 2:2], mixed[1:amount // 2 * 2:2]
    room = jnp.minimum(sizes[giver] - 1, bound - sizes[taker]) // 2
    room = jnp.where((giver == sequence[0]) | (taker == sequence[0]) | (sizes[taker] == 0), 0, jnp.maximum(room, 0))
    shifted = jax.random.randint(jax.random.fold_in(own, 4), (amount // 2,), 0, 1 << 20) % (room + 1)
    sizes = sizes.at[giver].add(-shifted).at[taker].add(shifted)
    members = jnp.searchsorted(jnp.cumsum(sizes), jnp.arange(rows * top), side="right").astype(jnp.int32)
    listing = members.reshape(top, rows).T
    listing = listing[jax.random.permutation(jax.random.fold_in(own, 1), rows)]
    rotation = jax.random.randint(jax.random.fold_in(own, 2), (rows, 1), 0, top)
    return jnp.take_along_axis(listing, (jnp.arange(top)[None, :] + rotation) % top, axis=1)


def shares(number_of, total, limit, slope, full):
    weights = [(1 << 20) // math.isqrt(rank ** slope) + 1 for rank in range(1, number_of + 1)]
    largest = limit if full else min(limit, max(-(-total // number_of), total * weights[0] // sum(weights)))
    least = 1 if total - largest >= number_of - 1 else 0
    counts, surplus = [largest] + [least] * (number_of - 1), total - largest - least * (number_of - 1)
    while surplus > 0:
        candidates = [i for i in range(1, number_of) if counts[i] < largest] or [i for i in range(1, number_of) if counts[i] < limit]
        pool, budget = sum([weights[i] for i in candidates]), surplus
        for i in candidates:
            extra = min(limit - counts[i], max(1, budget * weights[i] // pool), surplus)
            counts[i] = counts[i] + extra
            surplus = surplus - extra
    return np.array(counts)


def bell_draw(stream_key, shape, width, reach, cuts=(), kind=jnp.bfloat16):
    gain = block_scale(stream_key, shape, cuts, -0.22, 0.18) if cuts else 1.0
    values = jax.random.normal(stream_key, shape, jnp.float32) * width * gain
    return jnp.minimum(jnp.maximum(values, -reach), reach).astype(kind)


def setup_inputs(seed: int = 0) -> dict:
    key_of = jax.random.split(jax.random.key(seed), 8)
    tokens = bell_draw(key_of[0], (TOKENS, D), 1.0, 6.0, ((0, 256),))
    cotangent = bell_draw(key_of[1], (TOKENS, D), 1.0, 6.0, ((0, 256),))
    expert_ids_keys = jax.random.split(jax.random.fold_in(key_of[2], 1), TOKENS // TOK)
    expert_ids_turns = jax.random.permutation(jax.random.fold_in(key_of[2], 3), TOKENS // TOK)
    expert_ids = jax.vmap(lambda own, number: routed_block(jax.random.fold_in(key_of[2], 2), own, number, TOK, EXPERTS, TOP, CAP, 2))(expert_ids_keys, expert_ids_turns).reshape((TOKENS, TOP))
    gate_probs = jnp.clip(0.1 + 0.9 * jax.random.uniform(key_of[3], (TOKENS, TOP), jnp.float32) ** block_scale(key_of[3], (TOKENS, TOP), ((0, 256),), -0.2, 0.2), 0.1, 1.0)
    w_gate = bell_draw(key_of[4], (EXPERTS, D, FF), D ** -0.5, 0.125, ((0, 16), (2, 4)))
    w_up = bell_draw(key_of[5], (EXPERTS, D, FF), D ** -0.5, 0.125, ((0, 16), (2, 4)))
    w_down = bell_draw(key_of[6], (EXPERTS, FF, D), FF ** -0.5, 0.21875, ((0, 16), (1, 4)))
    return {"tokens": tokens, "cotangent": cotangent, "expert_ids": expert_ids, "gate_probs": gate_probs, "w_gate": w_gate, "w_up": w_up, "w_down": w_down}


def reference(tokens, cotangent, expert_ids, gate_probs, w_gate, w_up, w_down):
    groups = TOKENS // TOK
    rows_max = groups * CAP
    flat_ids = expert_ids.reshape(-1).astype(jnp.int32)
    count = flat_ids.shape[0]
    onehot = (flat_ids[:, None] == jnp.arange(EXPERTS, dtype=jnp.int32)[None, :]).astype(jnp.int32)
    ranks = jnp.sum((jnp.cumsum(onehot, 0) - onehot) * onehot, 1).astype(jnp.int32)
    dest = (flat_ids * rows_max + ranks).astype(jnp.int32)
    owners = (jnp.arange(count, dtype=jnp.int32) // TOP).astype(jnp.int32)
    source = jnp.full((EXPERTS * rows_max,), TOKENS, jnp.int32).at[dest].set(owners).reshape(EXPERTS, rows_max)
    weights = jnp.zeros((EXPERTS * rows_max,), jnp.float32).at[dest].set(gate_probs.reshape(-1).astype(jnp.float32)).reshape(EXPERTS, rows_max)
    padded_x = jnp.concatenate([tokens, jnp.zeros((1, D), tokens.dtype)], 0)
    padded_dy = jnp.concatenate([cotangent, jnp.zeros((1, D), cotangent.dtype)], 0)
    quarter = FF // N_TP

    def one_expert(items):
        rows, probs, weight_gate, weight_up, weight_down = items
        inputs = padded_x[rows]
        grads = padded_dy[rows]
        gate = jnp.dot(inputs, weight_gate, preferred_element_type=jnp.float32)
        up = jnp.dot(inputs, weight_up, preferred_element_type=jnp.float32)
        sigma = jax.nn.sigmoid(gate)
        active = gate * sigma
        hidden = (active * up).astype(jnp.bfloat16)
        back = jnp.dot(grads, weight_down.T, preferred_element_type=jnp.float32)
        prob_rows = jnp.sum(hidden.astype(jnp.float32) * back, 1)
        scale = probs[:, None]
        d_hidden = back * scale
        d_gate = (d_hidden * up * sigma * (1.0 + gate * (1.0 - sigma))).astype(jnp.bfloat16)
        d_up = (d_hidden * active).astype(jnp.bfloat16)
        scaled_hidden = (hidden.astype(jnp.float32) * scale).astype(jnp.bfloat16)
        grad_down = jnp.dot(scaled_hidden.T, grads, preferred_element_type=jnp.float32)
        grad_gate = jnp.dot(inputs.T, d_gate, preferred_element_type=jnp.float32)
        grad_up = jnp.dot(inputs.T, d_up, preferred_element_type=jnp.float32)
        total = jnp.zeros((rows_max, D), jnp.float32)
        for block in range(N_TP):
            lower = block * quarter
            upper = lower + quarter
            part = jnp.dot(d_gate[:, lower:upper], weight_gate[:, lower:upper].T, preferred_element_type=jnp.float32)
            part = part + jnp.dot(d_up[:, lower:upper], weight_up[:, lower:upper].T, preferred_element_type=jnp.float32)
            total = total + lax.optimization_barrier(part.astype(jnp.bfloat16)).astype(jnp.float32)
        return total.astype(jnp.bfloat16), prob_rows, grad_gate, grad_up, grad_down

    row_grad, prob_rows, grad_gate, grad_up, grad_down = lax.map(one_expert, (source, weights, w_gate, w_up, w_down))
    row_flat = row_grad.reshape(EXPERTS * rows_max, D)
    pair_dest = dest.reshape(TOKENS, TOP)
    summed = jnp.zeros((TOKENS, D), jnp.float32)
    for choice_k in range(TOP):
        summed = summed + row_flat[pair_dest[:, choice_k]].astype(jnp.float32)
    token_grad = summed.astype(jnp.bfloat16)
    prob_grad = prob_rows.reshape(-1)[dest].reshape(TOKENS, TOP)
    return token_grad, prob_grad, grad_gate, grad_up, grad_down
```

```python
import functools

import jax
import jax.numpy as jnp
from jax import lax
from jax.experimental import pallas as pl
from jax.experimental.pallas import tpu as pltpu
from jax.sharding import PartitionSpec as P

CAP = 10
ROWS = 16
SPARE = ROWS - CAP
LANES = 128
TAIL = 4 * LANES
BF = jnp.bfloat16
F32 = jnp.float32
MESH = pl.DeviceIdType.MESH
NT = ((1,), (1,))


def dot(a, b, dims=((1,), (0,)), precision=None):
    return lax.dot_general(
        a, b, (dims, ((), ())), preferred_element_type=F32, precision=precision
    )


def iota(shape, dim):
    return lax.broadcasted_iota(jnp.int32, shape, dim)


def hot(condition):
    return jnp.where(condition, 1.0, 0.0).astype(BF)


def kernel(
    nz, ny,
    tok, cot, ids_ref, probs_ref, wg, wu, wd,
    tg_ref, pg_ref, gg_ref, gu_ref, gd_ref,
    w, tq, cq, sb, rb, xs, ds, mx, md, gt, mgt, ch, cs, yl, yr, ip, xa, xl, xr, pk, rs, rr,
    ld, zs, zr, fs, fr, ms, mr, ps, pr, hs, hr, ys, yrs, vs, vr,
):
    t, z, island = lax.axis_index("tp"), lax.axis_index("ep"), lax.axis_index("island")
    y = lax.div(island, 2)
    core = island - 2 * y
    toks, quarter = tq.shape
    ff = wg.shape[0]
    m = nz * CAP
    n = nz * ROWS
    half = m // 2
    band = xs.shape[3]
    pairs = xs.shape[0]
    hz, hy = nz // 2, ny // 2
    fh = 3 * ff // 2
    part_a, part_b = pl.ds(0, fh), pl.ds(fh, fh)

    def tp_at(r):
        return {"tp": lax.rem(t + r, 4)}

    def ep_at(d):
        return {"ep": lax.rem(z + d, nz)}

    def y_at(d):
        return {"island": 2 * lax.rem(y + d, ny) + core}

    mate = {"island": 2 * y + 1 - core}

    def remote(src, dst, ssem, rsem, device):
        return pltpu.make_async_remote_copy(
            src_ref=src, dst_ref=dst, send_sem=ssem, recv_sem=rsem,
            device_id=device, device_id_type=MESH,
        )

    loads = [
        pltpu.make_async_copy(tok.at[:, pl.ds(pl.multiple_of(t * quarter, quarter), quarter)], tq, ld.at[0]),
        pltpu.make_async_copy(cot.at[:, pl.ds(pl.multiple_of(t * quarter, quarter), quarter)], cq, ld.at[1]),
        pltpu.make_async_copy(wg, w.at[pl.ds(0, ff)], ld.at[2]),
        pltpu.make_async_copy(wu, w.at[pl.ds(ff, ff)], ld.at[3]),
        pltpu.make_async_copy(wd, w.at[pl.ds(2 * ff, ff)], ld.at[4]),
    ]
    for copy in loads:
        copy.start()

    barrier = pltpu.get_barrier_semaphore()
    peers = [ep_at(d) for d in range(1, nz)] + [tp_at(r) for r in (1, 2, 3)]
    peers += [y_at(1), y_at(ny - 1), mate]
    for peer in peers:
        pl.semaphore_signal(barrier, inc=1, device_id=peer, device_id_type=MESH)

    ids = ids_ref[...]
    probs = probs_ref[...]
    named = hot(iota((nz, toks), 0) == ids)
    earlier = hot(iota((toks, toks), 0) < iota((toks, toks), 1))
    rank = jnp.sum(named.astype(F32) * dot(named, earlier), 0, keepdims=True)
    eye = iota((toks, toks), 0) == iota((toks, toks), 1)

    def column(row):
        return jnp.sum(jnp.where(eye, row, 0.0), 1, keepdims=True)

    probs_col = column(probs)
    ids_col = column(ids.astype(F32)).astype(jnp.int32)
    rank_col = column(rank).astype(jnp.int32)
    rank = rank.astype(jnp.int32)

    place = iota((n, toks), 0)
    block, row = lax.shift_right_logical(place, 4), place & (ROWS - 1)
    mine = block == ids
    pick_x = hot(mine & (row == rank))
    pick_d = hot(mine & (row == rank + CAP))
    piece = lax.shift_right_logical(row, 2)
    late = mine & ((row & 3) + SPARE == rank)
    pick_tail = [hot(late & (piece == c)) for c in range(4)]

    loads[0].wait()
    loads[1].wait()
    own_x = tq[...]
    own_d = (cq[...].astype(F32) * probs_col).astype(BF)
    main = dot(jnp.concatenate([pick_x, pick_d], 1), jnp.concatenate([own_x, own_d], 0))
    tail = dot(
        jnp.concatenate(pick_tail, 1),
        jnp.concatenate([own_d[:, LANES * c : LANES * (c + 1)] for c in range(4)], 0),
    )
    sb[:, :, 0:quarter] = main.astype(BF).reshape(nz, ROWS, quarter)
    sb[:, :, quarter : quarter + LANES] = tail.astype(BF).reshape(nz, ROWS, LANES)

    pl.semaphore_wait(barrier, len(peers))

    def hop(k):
        return hz + (1 - 2 * lax.rem(k, 2)) * lax.div(k + 1, 2)

    def z_send(k):
        d = hop(k)
        dst = lax.rem(z + d, nz)
        return remote(sb.at[dst], rb.at[t, z], zs.at[k], zr.at[k], ep_at(d))

    def z_source(k):
        return lax.rem(z - hop(k) + nz, nz)

    def z_recv(k):
        return remote(sb.at[0], rb.at[t, z_source(k)], zs.at[k], zr.at[k], ep_at(1))

    own_block = pltpu.make_async_copy(sb.at[z], rb.at[t, z], ld.at[5])
    own_block.start()

    def start_send(k, carry):
        z_send(k).start()
        return carry

    lax.fori_loop(0, nz - 1, start_send, 0)

    left_q, right_q, far_q = lax.rem(t + 3, 4), lax.rem(t + 1, 4), lax.rem(t + 2, 4)

    def pass_right(p, s):
        return remote(rb.at[t, s], rb.at[t, s], fs.at[0, p], fr.at[0, p], tp_at(1))

    def pass_left(p, s):
        return remote(rb.at[t, s], rb.at[t, s], fs.at[1, p], fr.at[1, p], tp_at(3))

    def from_left(p, s):
        return remote(rb.at[t, s], rb.at[left_q, s], fs.at[0, p], fr.at[0, p], tp_at(1))

    def from_right(p, s):
        return remote(rb.at[t, s], rb.at[right_q, s], fs.at[1, p], fr.at[1, p], tp_at(3))

    def onward(p, s, odd):
        q, to = (right_q, 3) if odd else (left_q, 1)
        return remote(rb.at[q, s], rb.at[q, s], fs.at[2, p], fr.at[2, p], tp_at(to))

    def from_far(p, s):
        return remote(rb.at[t, s], rb.at[far_q, s], fs.at[2, p], fr.at[2, p], tp_at(1))

    def share(p, s):
        pass_right(p, s).start()
        pass_left(p, s).start()

    def relay(p, s, odd):
        from_left(p, s).wait_recv()
        from_right(p, s).wait_recv()
        onward(p, s, odd).start()

    own_block.wait()
    share(0, z)
    z_recv(0).wait_recv()
    share(1, z_source(0))

    def gather(i, carry):
        for u in range(2):
            p = 2 * i + u
            z_recv(p - 1).wait_recv()
            share(p, z_source(p - 1))
        for u in range(2):
            p = 2 * i - 2 + u
            s = jnp.where(p == 0, z, z_source(jnp.maximum(p - 1, 0)))
            relay(p, s, u)
        return carry

    lax.fori_loop(1, hz, gather, 0)
    if nz > 2:
        relay(nz - 2, z_source(nz - 3), 0)
    else:
        relay(0, z, 0)
    relay(nz - 1, z_source(nz - 2), 1)
    from_far(0, z).wait_recv()

    def last(p, carry):
        from_far(p, z_source(p - 1)).wait_recv()
        return carry

    lax.fori_loop(1, nz, last, 0)

    rows = iota((m, n), 0)
    source = lax.shift_right_logical(rows * 6554, 16)
    slot = rows - CAP * source
    there = iota((m, n), 1)
    unpick_x = hot(there == ROWS * source + slot)
    unpick_d = hot((slot < SPARE) & (there == ROWS * source + CAP + slot))
    unpick_tail = [
        hot((slot >= SPARE) & (there == ROWS * source + 4 * c + slot - SPARE)) for c in range(4)
    ]
    unpick_main = jnp.concatenate([unpick_x, unpick_d], 0)
    unpick_tail = jnp.concatenate(unpick_tail, 0)
    per = quarter // band
    for q in range(4):
        got = rb[q].reshape(n, quarter + LANES)
        both = dot(unpick_main, got[:, 0:quarter])
        ends = dot(unpick_tail, got[:, quarter : quarter + LANES])
        ends = jnp.concatenate([ends[m * c : m * (c + 1)] for c in range(4)], 1)
        x_rows = both[0:m].astype(BF)
        d_rows = (both[m : 2 * m] + ends).astype(BF)
        for b in range(per):
            at = q * per + b
            xs[at // 2, at % 2] = x_rows[:, band * b : band * (b + 1)]
            ds[at // 2, at % 2] = d_rows[:, band * b : band * (b + 1)]

    mate_x = remote(xs.at[:, 1 - core], mx, ms.at[0], mr.at[0], mate)
    mate_d = remote(ds.at[:, 1 - core], md, ms.at[1], mr.at[1], mate)
    mate_g = remote(gt, mgt, ms.at[2], mr.at[2], mate)
    mate_x.start()
    mate_d.start()

    for copy in loads[2:]:
        copy.wait()
    gate_up = jnp.zeros((2 * ff, m), F32)
    back = jnp.zeros((ff, m), F32)
    for o in range(pairs):
        cols = pl.ds(2 * band * o, 2 * band)
        x_pair = jnp.concatenate([xs[o, 0], xs[o, 1]], 1)
        d_pair = jnp.concatenate([ds[o, 0], ds[o, 1]], 1)
        gate_up += dot(w[0 : 2 * ff, cols], x_pair, NT)
        back += dot(w[2 * ff : 3 * ff, cols], d_pair, NT)
    gate, up = gate_up[0:ff], gate_up[ff : 2 * ff]
    sigma = jax.nn.sigmoid(gate)
    active = gate * sigma
    hidden = (active * up).astype(BF)
    gt[0:ff, :] = (back * up * sigma * (1.0 + gate * (1.0 - sigma))).astype(BF)
    gt[ff : 2 * ff, :] = (back * active).astype(BF)
    gt[2 * ff : 3 * ff, :] = hidden
    mate_g.start()

    prob_row = jnp.sum(hidden.astype(F32) * back, 0, keepdims=True)
    in_source = iota((nz, m), 0) == lax.shift_right_logical(iota((nz, m), 1) * 6554, 16)
    at_row = iota((m, LANES), 0)
    at_slot = iota((m, LANES), 1) == at_row - CAP * lax.shift_right_logical(at_row * 6554, 16)
    pk[0] = dot(
        jnp.where(in_source, prob_row, 0.0), jnp.where(at_slot, 1.0, 0.0),
        precision=lax.Precision.HIGHEST,
    )
    prob_sends = [remote(pk.at[0], pk.at[r], ps.at[r], pr.at[r], tp_at(r)) for r in (1, 2, 3)]
    for copy in prob_sends:
        copy.start()

    eye_m = hot(iota((m, m), 0) == iota((m, m), 1))
    d_rows = dot(eye_m, gt[0 : 2 * ff, :], NT).astype(BF)

    def input_part(r):
        q = lax.rem(t + r, 4)
        cols = pl.ds(pl.multiple_of(q * quarter, quarter), quarter)
        ip[r] = dot(d_rows, w[0 : 2 * ff, cols]).astype(BF)

    low, high = pl.ds(0, half), pl.ds(half, half)
    to_right = [
        remote(ip.at[2, low], xa.at[0], hs.at[0, 0], hr.at[0, 0], tp_at(1)),
        remote(ip.at[1, high], xl.at[high], hs.at[0, 1], hr.at[0, 1], tp_at(1)),
        remote(ip.at[1, low], xl.at[low], hs.at[0, 2], hr.at[0, 2], tp_at(1)),
    ]
    to_left = [
        remote(ip.at[2, high], xa.at[1], hs.at[1, 0], hr.at[1, 0], tp_at(3)),
        remote(ip.at[3, low], xr.at[low], hs.at[1, 1], hr.at[1, 1], tp_at(3)),
        remote(ip.at[3, high], xr.at[high], hs.at[1, 2], hr.at[1, 2], tp_at(3)),
    ]
    input_part(2)
    to_right[0].start()
    to_left[0].start()

    def weight_part(j):
        o = lax.rem(y + j, ny)
        x_own, d_own, x_mate, d_mate = xs[o, core], ds[o, core], mx[o], md[o]
        ch[j, 0 : 2 * ff, :] = dot(gt[0 : 2 * ff, :], x_own) + dot(mgt[0 : 2 * ff, :], x_mate)
        ch[j, 2 * ff : 3 * ff, :] = dot(gt[2 * ff : 3 * ff, :], d_own) + dot(
            mgt[2 * ff : 3 * ff, :], d_mate
        )

    def y_copy(side, dist, part):
        j = dist if side == 0 else ny - dist
        where = part_b if part else part_a
        into = (yl, yr)[side]
        return remote(
            cs.at[j, where], into.at[dist - 1, where],
            ys.at[side, dist, part], yrs.at[side, dist, part], y_at(1 if side == 0 else ny - 1),
        )

    def y_step(side, dist, part):
        j = dist if side == 0 else ny - dist
        where = part_b if part else part_a
        alone = dist == hy or (dist == hy - 1 and part == 1 - side)
        if alone:
            cs[j, where, :] = ch[j, where, :].astype(BF)
        else:
            y_copy(side, dist + 1, part).wait_recv()
            came = (yl, yr)[side][dist, where, :].astype(F32)
            cs[j, where, :] = (ch[j, where, :] + came).astype(BF)
        y_copy(side, dist, part).start()

    mate_x.wait_recv()
    mate_d.wait_recv()
    mate_g.wait_recv()
    weight_part(hy)
    y_step(0, hy, 0)
    y_step(1, hy, 1)
    weight_part(hy - 1)
    y_step(0, hy - 1, 1)
    weight_part(ny - hy + 1)
    y_step(1, hy - 1, 0)

    input_part(1)
    to_right[1].start()
    input_part(3)
    to_left[1].start()
    for dist in range(hy - 2, 0, -1):
        weight_part(dist)
        weight_part(ny - dist)
    to_right[0].wait_recv()
    ip[1, low, :] = (ip[1, low, :].astype(F32) + xa[0].astype(F32)).astype(BF)
    to_right[2].start()
    to_left[0].wait_recv()
    ip[3, high, :] = (ip[3, high, :].astype(F32) + xa[1].astype(F32)).astype(BF)
    to_left[2].start()
    y_step(0, hy - 1, 0)
    y_step(1, hy - 1, 1)
    input_part(0)
    weight_part(0)
    if hy > 2:
        y_step(0, hy - 2, 1)
        y_step(1, hy - 2, 0)

    for copy in prob_sends:
        copy.wait_recv()
    prob = (pk[0] + pk[1]) + (pk[2] + pk[3])
    prob_high = prob.astype(BF)
    prob_low = (prob - prob_high.astype(F32)).astype(BF)
    to = iota((n, m), 0)
    block, row = lax.shift_right_logical(to, 4), to & (ROWS - 1)
    first = CAP * block
    frm = iota((n, m), 1)
    pack = hot((row < CAP) & (frm == first + row))
    pack_0 = hot((row >= CAP) & (frm == first + row - CAP))
    pack_1 = hot((row >= CAP) & (row < ROWS - 2) & (frm == first + row - CAP + SPARE))
    to = iota((n, nz), 0)
    block, row = lax.shift_right_logical(to, 4), to & (ROWS - 1)
    same = block == iota((n, nz), 1)
    pack_high, pack_low = hot(same & (row == CAP)), hot(same & (row == CAP + 1))
    to_right[1].wait_recv()
    to_left[1].wait_recv()
    to_right[2].wait_recv()
    to_left[2].wait_recv()
    summed = (
        ip[0].astype(F32) + (xl[...].astype(F32) + xr[...].astype(F32))
    ).astype(BF)
    ends = summed[:, 3 * LANES : 4 * LANES]
    packed = dot(pack, summed[:, 0 : 3 * LANES])
    packed = packed + jnp.concatenate(
        [dot(pack_0, ends), dot(pack_1, ends), dot(pack_high, prob_high) + dot(pack_low, prob_low)], 1
    )
    rs[...] = packed.astype(BF).reshape(nz, ROWS, 3 * LANES)

    def back_send(k):
        d = hop(k)
        dst = lax.rem(z + d, nz)
        return remote(rs.at[dst], rr.at[z], vs.at[k], vr.at[k], ep_at(d))

    def back_recv(k):
        return remote(rs.at[0], rr.at[z_source(k)], vs.at[k], vr.at[k], ep_at(1))

    def start_back(k, carry):
        back_send(k).start()
        return carry

    lax.fori_loop(0, nz - 1, start_back, 0)
    own_back = pltpu.make_async_copy(rs.at[z], rr.at[z], ld.at[6])
    own_back.start()

    for dist in range(hy - 2, 0, -1):
        if dist < hy - 2:
            y_step(0, dist, 1)
            y_step(1, dist, 0)
        y_step(0, dist, 0)
        y_step(1, dist, 1)
    for part in (0, 1):
        for side in (0, 1):
            y_copy(side, 1, 1 - part if side == 0 else part).wait_recv()
    total = ch[0] + (yl[0].astype(F32) + yr[0].astype(F32))
    gg_ref[...] = total[0:ff]
    gu_ref[...] = total[ff : 2 * ff]
    gd_ref[...] = total[2 * ff : 3 * ff]

    at = iota((toks, n), 1)
    block, row = lax.shift_right_logical(at, 4), at & (ROWS - 1)
    mine = block == ids_col
    take = hot(mine & (row == rank_col))
    take_0 = hot(mine & (row == rank_col + CAP) & (rank_col < SPARE))
    take_1 = hot(mine & (row == rank_col + CAP - SPARE) & (rank_col >= SPARE))
    take_high, take_low = hot(mine & (row == CAP)), hot(mine & (row == CAP + 1))

    def wait_back(k, carry):
        back_recv(k).wait_recv()
        return carry

    lax.fori_loop(0, nz - 1, wait_back, 0)
    own_back.wait()
    got = rr[...].reshape(n, 3 * LANES)
    tg_ref[:, 0 : 3 * LANES] = dot(take, got).astype(BF)
    tg_ref[:, 3 * LANES : 4 * LANES] = (
        dot(take_0, got[:, 0:LANES]) + dot(take_1, got[:, LANES : 2 * LANES])
    ).astype(BF)
    ends = got[:, 2 * LANES : 3 * LANES]
    chosen = iota((toks, LANES), 1) == rank_col
    value = jnp.where(chosen, dot(take_high, ends) + dot(take_low, ends), 0.0)
    value = jnp.sum(value, 1, keepdims=True) / probs_col
    pg_ref[...] = jnp.sum(jnp.where(eye, value, 0.0), 0, keepdims=True)

    def left_z(k, carry):
        z_send(k).wait_send()
        back_send(k).wait_send()
        return carry

    lax.fori_loop(0, nz - 1, left_z, 0)

    def left_x(i, carry):
        for u in range(2):
            p = 2 * i + u
            pass_right(p, z).wait_send()
            pass_left(p, z).wait_send()
            onward(p, z, u).wait_send()
        return carry

    lax.fori_loop(0, hz, left_x, 0)
    for copy in [mate_x, mate_d, mate_g] + prob_sends + to_right + to_left:
        copy.wait_send()
    for side in (0, 1):
        y_copy(side, hy, side).wait_send()
        for dist in range(hy - 1, 0, -1):
            for part in (0, 1):
                y_copy(side, dist, part).wait_send()


def shards(tokens, cotangent, expert_ids, gate_probs, w_gate, w_up, w_down):
    toks, width = tokens.shape
    ff = w_down.shape[1]
    nz, ny = lax.axis_size("ep"), lax.axis_size("island") // 2
    quarter, band = width // 4, width // (2 * ny)
    m = nz * CAP
    wide = quarter + LANES
    hy, hz = ny // 2, nz // 2
    hbm = pl.BlockSpec(memory_space=pl.ANY)
    vmem = pl.BlockSpec(memory_space=pltpu.VMEM)
    dma = pltpu.SemaphoreType.DMA
    token_grad, prob_grad, grad_gate, grad_up, grad_down = pl.pallas_call(
        functools.partial(kernel, nz, ny),
        out_shape=(
            jax.ShapeDtypeStruct((toks, quarter), BF),
            jax.ShapeDtypeStruct((1, toks), F32),
            jax.ShapeDtypeStruct((ff, band), F32),
            jax.ShapeDtypeStruct((ff, band), F32),
            jax.ShapeDtypeStruct((ff, band), F32),
        ),
        in_specs=[hbm, hbm, vmem, vmem, hbm, hbm, hbm],
        out_specs=(vmem,) * 5,
        scratch_shapes=[
            pltpu.VMEM((3 * ff, width), BF),
            pltpu.VMEM((toks, quarter), BF),
            pltpu.VMEM((toks, quarter), BF),
            pltpu.VMEM((nz, ROWS, wide), BF),
            pltpu.VMEM((4, nz, ROWS, wide), BF),
            pltpu.VMEM((ny, 2, m, band), BF),
            pltpu.VMEM((ny, 2, m, band), BF),
            pltpu.VMEM((ny, m, band), BF),
            pltpu.VMEM((ny, m, band), BF),
            pltpu.VMEM((3 * ff, m), BF),
            pltpu.VMEM((3 * ff, m), BF),
            pltpu.VMEM((ny, 3 * ff, band), F32),
            pltpu.VMEM((ny, 3 * ff, band), BF),
            pltpu.VMEM((hy, 3 * ff, band), BF),
            pltpu.VMEM((hy, 3 * ff, band), BF),
            pltpu.VMEM((4, m, quarter), BF),
            pltpu.VMEM((2, m // 2, quarter), BF),
            pltpu.VMEM((m, quarter), BF),
            pltpu.VMEM((m, quarter), BF),
            pltpu.VMEM((4, nz, LANES), F32),
            pltpu.VMEM((nz, ROWS, 3 * LANES), BF),
            pltpu.VMEM((nz, ROWS, 3 * LANES), BF),
            dma((7,)),
            dma((nz,)), dma((nz,)),
            dma((3, nz)), dma((3, nz)),
            dma((3,)), dma((3,)),
            dma((4,)), dma((4,)),
            dma((2, 3)), dma((2, 3)),
            dma((2, hy + 1, 2)), dma((2, hy + 1, 2)),
            dma((nz,)), dma((nz,)),
        ],
        compiler_params=pltpu.CompilerParams(
            collective_id=0, has_side_effects=True, vmem_limit_bytes=56 * 1024 * 1024
        ),
    )(
        tokens, cotangent,
        expert_ids.reshape(1, toks), gate_probs.reshape(1, toks),
        w_gate[0].T, w_up[0].T, w_down[0],
    )
    return (
        token_grad, prob_grad.reshape(toks, 1),
        grad_gate.T[None], grad_up.T[None], grad_down[None],
    )


def solution(mesh):
    rows = P(("island", "ep"), None)
    in_specs = (rows, rows, rows, rows, P("ep", None, "tp"), P("ep", None, "tp"), P("ep", "tp", None))
    out_specs = (
        P(("island", "ep"), "tp"), rows,
        P("ep", "island", "tp"), P("ep", "island", "tp"), P("ep", "tp", "island"),
    )
    return jax.shard_map(shards, mesh=mesh, in_specs=in_specs, out_specs=out_specs, check_vma=False)
```

```python
import functools

import jax
import jax.numpy as jnp
from jax import lax
from jax.experimental import pallas as pl
from jax.experimental.pallas import tpu as pltpu
from jax.sharding import PartitionSpec as P

CAP = 10
ROWS = 16
SPARE = ROWS - CAP
LANES = 128
TAIL = 4 * LANES
BF = jnp.bfloat16
F32 = jnp.float32
MESH = pl.DeviceIdType.MESH
NT = ((1,), (1,))


def dot(a, b, dims=((1,), (0,)), precision=None):
    return lax.dot_general(
        a, b, (dims, ((), ())), preferred_element_type=F32, precision=precision
    )


def iota(shape, dim):
    return lax.broadcasted_iota(jnp.int32, shape, dim)


def hot(condition):
    return jnp.where(condition, 1.0, 0.0).astype(BF)


def kernel(
    nz, ny,
    tok, cot, ids_hbm, probs_hbm, wg, wu, wd,
    tg_ref, pg_ref, gg_ref, gu_ref, gd_ref,
    ids_ref, probs_ref, w, tq, cq, sb, rb, xs, ds, mx, md, gt, mgt, ch, cs, yl, yr, ip, xa, xl, xr, pk, rs, rr,
    ld, zs, zr, fs, fr, ms, mr, ps, pr, hs, hr, ys, yrs, vs, vr,
):
    t, z, island = lax.axis_index("tp"), lax.axis_index("ep"), lax.axis_index("island")
    y = lax.div(island, 2)
    core = island - 2 * y
    toks, quarter = tq.shape
    ff = wg.shape[0]
    m = nz * CAP
    n = nz * ROWS
    half = m // 2
    band = xs.shape[3]
    pairs = xs.shape[0]
    hz, hy = nz // 2, ny // 2
    piece_rows = 3 * ff // 4

    def tp_at(r):
        return {"tp": lax.rem(t + r, 4)}

    def ep_at(d):
        return {"ep": lax.rem(z + d, nz)}

    def y_at(d):
        return {"island": 2 * lax.rem(y + d, ny) + core}

    mate = {"island": 2 * y + 1 - core}

    def remote(src, dst, ssem, rsem, device):
        return pltpu.make_async_remote_copy(
            src_ref=src, dst_ref=dst, send_sem=ssem, recv_sem=rsem,
            device_id=device, device_id_type=MESH,
        )

    loads = [
        pltpu.make_async_copy(ids_hbm, ids_ref, ld.at[7]),
        pltpu.make_async_copy(probs_hbm, probs_ref, ld.at[8]),
        pltpu.make_async_copy(tok.at[:, pl.ds(pl.multiple_of(t * quarter, quarter), quarter)], tq, ld.at[0]),
        pltpu.make_async_copy(cot.at[:, pl.ds(pl.multiple_of(t * quarter, quarter), quarter)], cq, ld.at[1]),
        pltpu.make_async_copy(wg, w.at[pl.ds(0, ff)], ld.at[2]),
        pltpu.make_async_copy(wu, w.at[pl.ds(ff, ff)], ld.at[3]),
        pltpu.make_async_copy(wd, w.at[pl.ds(2 * ff, ff)], ld.at[4]),
    ]
    for copy in loads:
        copy.start()

    barrier = pltpu.get_barrier_semaphore()
    peers = [ep_at(d) for d in range(1, nz)] + [tp_at(r) for r in (1, 2, 3)]
    peers += [y_at(1), y_at(ny - 1), mate]
    for peer in peers:
        pl.semaphore_signal(barrier, inc=1, device_id=peer, device_id_type=MESH)

    loads[0].wait()
    loads[1].wait()

    ids = ids_ref[...]
    probs = probs_ref[...]
    named = hot(iota((nz, toks), 0) == ids)
    earlier = hot(iota((toks, toks), 0) < iota((toks, toks), 1))
    rank = jnp.sum(named.astype(F32) * dot(named, earlier), 0, keepdims=True)
    eye = iota((toks, toks), 0) == iota((toks, toks), 1)

    def column(row):
        return jnp.sum(jnp.where(eye, row, 0.0), 1, keepdims=True)

    probs_col = column(probs)
    ids_col = column(ids.astype(F32)).astype(jnp.int32)
    rank_col = column(rank).astype(jnp.int32)
    rank = rank.astype(jnp.int32)

    place = iota((n, toks), 0)
    block, row = lax.shift_right_logical(place, 4), place & (ROWS - 1)
    mine = block == ids
    pick_x = hot(mine & (row == rank))
    pick_d = hot(mine & (row == rank + CAP))
    piece = lax.shift_right_logical(row, 2)
    late = mine & ((row & 3) + SPARE == rank)
    pick_tail = [hot(late & (piece == c)) for c in range(4)]

    loads[2].wait()
    loads[3].wait()
    own_x = tq[...]
    own_d = (cq[...].astype(F32) * probs_col).astype(BF)
    main = dot(jnp.concatenate([pick_x, pick_d], 1), jnp.concatenate([own_x, own_d], 0))
    tail = dot(
        jnp.concatenate(pick_tail, 1),
        jnp.concatenate([own_d[:, LANES * c : LANES * (c + 1)] for c in range(4)], 0),
    )
    sb[:, :, 0:quarter] = main.astype(BF).reshape(nz, ROWS, quarter)
    sb[:, :, quarter : quarter + LANES] = tail.astype(BF).reshape(nz, ROWS, LANES)

    pl.semaphore_wait(barrier, len(peers))

    def hop(k):
        j = lax.div(k, 2) + 1
        return jnp.where(lax.rem(k, 2) == 0, j, nz - j)

    def z_send(k):
        d = hop(k)
        return remote(sb.at[lax.rem(z + d, nz)], rb.at[t, k + 1], zs.at[k], zr.at[k], ep_at(d))

    def z_recv(k):
        return remote(sb.at[0], rb.at[t, k + 1], zs.at[k], zr.at[k], ep_at(1))

    own_block = pltpu.make_async_copy(sb.at[z], rb.at[t, 0], ld.at[5])
    own_block.start()

    def start_send(k, carry):
        z_send(k).start()
        return carry

    lax.fori_loop(0, nz - 1, start_send, 0)

    left_q, right_q, far_q = lax.rem(t + 3, 4), lax.rem(t + 1, 4), lax.rem(t + 2, 4)

    def pass_right(p):
        return remote(rb.at[t, p], rb.at[t, p], fs.at[0, p], fr.at[0, p], tp_at(1))

    def pass_left(p):
        return remote(rb.at[t, p], rb.at[t, p], fs.at[1, p], fr.at[1, p], tp_at(3))

    def from_left(p):
        return remote(rb.at[t, p], rb.at[left_q, p], fs.at[0, p], fr.at[0, p], tp_at(1))

    def from_right(p):
        return remote(rb.at[t, p], rb.at[right_q, p], fs.at[1, p], fr.at[1, p], tp_at(3))

    def onward(p, odd):
        q, to = (right_q, 3) if odd else (left_q, 1)
        return remote(rb.at[q, p], rb.at[q, p], fs.at[2, p], fr.at[2, p], tp_at(to))

    def from_far(p):
        return remote(rb.at[t, p], rb.at[far_q, p], fs.at[2, p], fr.at[2, p], tp_at(1))

    def share(p):
        pass_right(p).start()
        pass_left(p).start()

    def relay(p, odd):
        from_left(p).wait_recv()
        from_right(p).wait_recv()
        onward(p, odd).start()

    own_block.wait()
    share(0)
    z_recv(0).wait_recv()
    share(1)

    def gather(i, carry):
        for u in range(2):
            p = 2 * i + u
            z_recv(p - 1).wait_recv()
            share(p)
        for u in range(2):
            relay(2 * i - 2 + u, u)
        return carry

    lax.fori_loop(1, hz, gather, 0)
    relay(nz - 2, 0)
    relay(nz - 1, 1)

    def last(p, carry):
        from_far(p).wait_recv()
        return carry

    lax.fori_loop(0, nz, last, 0)

    rows = iota((m, n), 0)
    source = lax.shift_right_logical(rows * 6554, 16)
    slot = rows - CAP * source
    there = iota((m, n), 1)
    unpick_x = hot(there == ROWS * source + slot)
    unpick_d = hot((slot < SPARE) & (there == ROWS * source + CAP + slot))
    unpick_tail = [
        hot((slot >= SPARE) & (there == ROWS * source + 4 * c + slot - SPARE)) for c in range(4)
    ]
    unpick_main = jnp.concatenate([unpick_x, unpick_d], 0)
    unpick_tail = jnp.concatenate(unpick_tail, 0)
    per = quarter // band
    for q in range(4):
        got = rb[q].reshape(n, quarter + LANES)
        both = dot(unpick_main, got[:, 0:quarter])
        ends = dot(unpick_tail, got[:, quarter : quarter + LANES])
        ends = jnp.concatenate([ends[m * c : m * (c + 1)] for c in range(4)], 1)
        x_rows = both[0:m].astype(BF)
        d_rows = (both[m : 2 * m] + ends).astype(BF)
        for b in range(per):
            at = q * per + b
            xs[at // 2, at % 2] = x_rows[:, band * b : band * (b + 1)]
            ds[at // 2, at % 2] = d_rows[:, band * b : band * (b + 1)]

    mate_x = remote(xs.at[:, 1 - core], mx, ms.at[0], mr.at[0], mate)
    mate_d = remote(ds.at[:, 1 - core], md, ms.at[1], mr.at[1], mate)
    mate_g = remote(gt, mgt, ms.at[2], mr.at[2], mate)
    mate_x.start()
    mate_d.start()

    for copy in loads[4:]:
        copy.wait()
    x_all = jnp.concatenate([xs[o, c] for o in range(pairs) for c in range(2)], 1)
    d_all = jnp.concatenate([ds[o, c] for o in range(pairs) for c in range(2)], 1)
    gate_up = dot(w[0 : 2 * ff, :], x_all, NT)
    back = dot(w[2 * ff : 3 * ff, :], d_all, NT)
    gate, up = gate_up[0:ff], gate_up[ff : 2 * ff]
    sigma = jax.nn.sigmoid(gate)
    active = gate * sigma
    hidden = (active * up).astype(BF)
    gt[0:ff, :] = (back * up * sigma * (1.0 + gate * (1.0 - sigma))).astype(BF)
    gt[ff : 2 * ff, :] = (back * active).astype(BF)
    gt[2 * ff : 3 * ff, :] = hidden
    mate_g.start()

    eye_m = hot(iota((m, m), 0) == iota((m, m), 1))
    d_rows = dot(eye_m, gt[0 : 2 * ff, :], NT).astype(BF)

    def input_part(r):
        q = lax.rem(t + r, 4)
        cols = pl.ds(pl.multiple_of(q * quarter, quarter), quarter)
        ip[r] = dot(d_rows, w[0 : 2 * ff, cols]).astype(BF)

    cut = half * 3 // 5
    parts = [
        (pl.ds(0, half - cut), pl.ds(half - cut, cut)),
        (pl.ds(half, cut), pl.ds(half + cut, half - cut)),
    ]

    def tp_copies(g):
        one, two = parts[g]
        to_right = [
            remote(ip.at[2, one], xa.at[0, one], hs.at[0, g, 0], hr.at[0, g, 0], tp_at(1)),
            remote(ip.at[1, two], xl.at[two], hs.at[0, g, 1], hr.at[0, g, 1], tp_at(1)),
            remote(ip.at[1, one], xl.at[one], hs.at[0, g, 2], hr.at[0, g, 2], tp_at(1)),
        ]
        to_left = [
            remote(ip.at[2, two], xa.at[1, two], hs.at[1, g, 0], hr.at[1, g, 0], tp_at(3)),
            remote(ip.at[3, one], xr.at[one], hs.at[1, g, 1], hr.at[1, g, 1], tp_at(3)),
            remote(ip.at[3, two], xr.at[two], hs.at[1, g, 2], hr.at[1, g, 2], tp_at(3)),
        ]
        return to_right, to_left

    tp_sums = [tp_copies(0), tp_copies(1)]

    def tp_start(g, i):
        for side in (0, 1):
            tp_sums[g][side][i].start()

    def tp_pass(g):
        one, two = parts[g]
        tp_sums[g][0][0].wait_recv()
        ip[1, one, :] = (ip[1, one, :].astype(F32) + xa[0, one, :].astype(F32)).astype(BF)
        tp_sums[g][0][2].start()
        tp_sums[g][1][0].wait_recv()
        ip[3, two, :] = (ip[3, two, :].astype(F32) + xa[1, two, :].astype(F32)).astype(BF)
        tp_sums[g][1][2].start()

    def weight_part(*js):
        def cat(blocks):
            return blocks[0] if len(blocks) == 1 else jnp.concatenate(blocks, 1)

        os = [lax.rem(y + j, ny) for j in js]
        top = dot(gt[0 : 2 * ff, :], cat([xs[o, core] for o in os]))
        top = top + dot(mgt[0 : 2 * ff, :], cat([mx[o] for o in os]))
        low = dot(gt[2 * ff : 3 * ff, :], cat([ds[o, core] for o in os]))
        low = low + dot(mgt[2 * ff : 3 * ff, :], cat([md[o] for o in os]))
        for i, j in enumerate(js):
            ch[j, 0 : 2 * ff, :] = top[:, band * i : band * (i + 1)]
            ch[j, 2 * ff : 3 * ff, :] = low[:, band * i : band * (i + 1)]

    def y_copy(side, dist, part):
        j = dist if side == 0 else ny - dist
        where = pl.ds(part * piece_rows, piece_rows)
        into = (yl, yr)[side]
        return remote(
            cs.at[j, where], into.at[dist - 1, where],
            ys.at[side, dist, part], yrs.at[side, dist, part], y_at(1 if side == 0 else ny - 1),
        )

    far_parts, near_parts = ((0, 1), (2, 3)), ((2, 3), (0, 1))

    def y_step(side, dist, part):
        j = dist if side == 0 else ny - dist
        where = pl.ds(part * piece_rows, piece_rows)
        if dist == hy or (dist == hy - 1 and part in near_parts[side]):
            cs[j, where, :] = ch[j, where, :].astype(BF)
        else:
            y_copy(side, dist + 1, part).wait_recv()
            came = (yl, yr)[side][dist, where, :].astype(F32)
            cs[j, where, :] = (ch[j, where, :] + came).astype(BF)
        y_copy(side, dist, part).start()

    def y_steps(dist, parts):
        for i in range(2):
            for side in (0, 1):
                y_step(side, dist, parts[side][i])

    input_part(2)
    tp_start(1, 0)
    tp_start(0, 0)
    input_part(1)
    input_part(3)
    tp_start(1, 1)

    mate_x.wait_recv()
    mate_d.wait_recv()
    mate_g.wait_recv()
    weight_part(hy)
    y_steps(hy, far_parts)
    weight_part(hy - 1, ny - hy + 1)
    y_steps(hy - 1, near_parts)
    tp_pass(1)
    tp_start(0, 1)
    tp_pass(0)

    prob_row = jnp.sum(hidden.astype(F32) * back, 0, keepdims=True)
    in_source = iota((nz, m), 0) == lax.shift_right_logical(iota((nz, m), 1) * 6554, 16)
    at_row = iota((m, LANES), 0)
    at_slot = iota((m, LANES), 1) == at_row - CAP * lax.shift_right_logical(at_row * 6554, 16)
    pk[0] = dot(
        jnp.where(in_source, prob_row, 0.0), jnp.where(at_slot, 1.0, 0.0),
        precision=lax.Precision.HIGHEST,
    )
    prob_sends = [remote(pk.at[0], pk.at[r], ps.at[r], pr.at[r], tp_at(r)) for r in (1, 2, 3)]
    for copy in prob_sends:
        copy.start()
    input_part(0)
    y_steps(hy - 1, far_parts)
    for dist in range(hy - 2, 0, -1):
        weight_part(dist, ny - dist)

    for copy in prob_sends:
        copy.wait_recv()
    prob = (pk[0] + pk[1]) + (pk[2] + pk[3])
    prob_high = prob.astype(BF)
    prob_low = (prob - prob_high.astype(F32)).astype(BF)
    to = iota((n // 2, half), 0)
    block, row = lax.shift_right_logical(to, 4), to & (ROWS - 1)
    first = CAP * block
    frm = iota((n // 2, half), 1)
    pack = hot((row < CAP) & (frm == first + row))
    pack_0 = hot((row >= CAP) & (frm == first + row - CAP))
    pack_1 = hot((row >= CAP) & (row < ROWS - 2) & (frm == first + row - CAP + SPARE))
    to = iota((n // 2, nz), 0)
    block, row = lax.shift_right_logical(to, 4), to & (ROWS - 1)

    def back_send(k):
        d = hop(k)
        return remote(rs.at[k + 1], rr.at[z], vs.at[k], vr.at[k], ep_at(nz - d))

    def back_recv(k):
        return remote(rs.at[0], rr.at[lax.rem(z + hop(k), nz)], vs.at[k], vr.at[k], ep_at(1))

    def start_back(k, carry):
        back_send(k).start()
        return carry

    def send_back(g):
        for i in (1, 2):
            for side in (0, 1):
                tp_sums[g][side][i].wait_recv()
        here = pl.ds(g * half, half)
        summed = (
            ip[0, here, :].astype(F32) + (xl[here, :].astype(F32) + xr[here, :].astype(F32))
        ).astype(BF)
        ends = summed[:, 3 * LANES : 4 * LANES]
        same = block + g * hz == iota((n // 2, nz), 1)
        extra = dot(hot(same & (row == CAP)), prob_high) + dot(hot(same & (row == CAP + 1)), prob_low)
        packed = dot(pack, summed[:, 0 : 3 * LANES])
        packed = packed + jnp.concatenate([dot(pack_0, ends), dot(pack_1, ends), extra], 1)
        rs[pl.ds(g * hz, hz)] = packed.astype(BF).reshape(hz, ROWS, 3 * LANES)
        lax.fori_loop(hz - 1 if g else 0, nz - 1 if g else hz - 1, start_back, 0)

    send_back(1)
    if hy > 2:
        y_steps(hy - 2, near_parts)
    send_back(0)
    own_back = pltpu.make_async_copy(rs.at[0], rr.at[z], ld.at[6])
    own_back.start()
    for dist in range(hy - 2, 0, -1):
        if dist < hy - 2:
            y_steps(dist, near_parts)
        y_steps(dist, far_parts)
    weight_part(0)
    for parts_at in (near_parts, far_parts):
        for i in range(2):
            for side in (0, 1):
                y_copy(side, 1, parts_at[side][i]).wait_recv()
    total = ch[0] + (yl[0].astype(F32) + yr[0].astype(F32))
    gg_ref[...] = total[0:ff]
    gu_ref[...] = total[ff : 2 * ff]
    gd_ref[...] = total[2 * ff : 3 * ff]

    at = iota((toks, n), 1)
    block, row = lax.shift_right_logical(at, 4), at & (ROWS - 1)
    mine = block == ids_col
    take = hot(mine & (row == rank_col))
    take_0 = hot(mine & (row == rank_col + CAP) & (rank_col < SPARE))
    take_1 = hot(mine & (row == rank_col + CAP - SPARE) & (rank_col >= SPARE))
    take_high, take_low = hot(mine & (row == CAP)), hot(mine & (row == CAP + 1))

    def wait_back(k, carry):
        back_recv(k).wait_recv()
        return carry

    lax.fori_loop(0, nz - 1, wait_back, 0)
    own_back.wait()
    got = rr[...].reshape(n, 3 * LANES)
    tg_ref[:, 0 : 3 * LANES] = dot(take, got).astype(BF)
    tg_ref[:, 3 * LANES : 4 * LANES] = (
        dot(take_0, got[:, 0:LANES]) + dot(take_1, got[:, LANES : 2 * LANES])
    ).astype(BF)
    ends = got[:, 2 * LANES : 3 * LANES]
    chosen = iota((toks, LANES), 1) == rank_col
    value = jnp.where(chosen, dot(take_high, ends) + dot(take_low, ends), 0.0)
    value = jnp.sum(value, 1, keepdims=True) / probs_col
    pg_ref[...] = jnp.sum(jnp.where(eye, value, 0.0), 0, keepdims=True)

    def left_z(k, carry):
        z_send(k).wait_send()
        back_send(k).wait_send()
        return carry

    lax.fori_loop(0, nz - 1, left_z, 0)

    def left_x(i, carry):
        for u in range(2):
            p = 2 * i + u
            pass_right(p).wait_send()
            pass_left(p).wait_send()
            onward(p, u).wait_send()
        return carry

    lax.fori_loop(0, hz, left_x, 0)
    for copy in [mate_x, mate_d, mate_g] + prob_sends:
        copy.wait_send()
    for group in tp_sums:
        for side in group:
            for copy in side:
                copy.wait_send()
    for side in (0, 1):
        for part in far_parts[side]:
            y_copy(side, hy, part).wait_send()
        for dist in range(hy - 1, 0, -1):
            for part in range(4):
                y_copy(side, dist, part).wait_send()


def publish(*refs):
    copies = [pltpu.make_async_copy(refs[i], refs[i + 5], refs[10].at[i]) for i in range(5)]
    for copy in copies:
        copy.start()
    for copy in copies:
        copy.wait()


def shards(tokens, cotangent, expert_ids, gate_probs, w_gate, w_up, w_down):
    toks, width = tokens.shape
    ff = w_down.shape[1]
    nz, ny = lax.axis_size("ep"), lax.axis_size("island") // 2
    quarter, band = width // 4, width // (2 * ny)
    m = nz * CAP
    wide = quarter + LANES
    hy, hz = ny // 2, nz // 2
    hbm = pl.BlockSpec(memory_space=pltpu.HBM)
    vmem = pl.BlockSpec(memory_space=pltpu.VMEM)
    dma = pltpu.SemaphoreType.DMA
    shapes = (
        jax.ShapeDtypeStruct((toks, quarter), BF),
        jax.ShapeDtypeStruct((1, toks), F32),
        jax.ShapeDtypeStruct((ff, band), F32),
        jax.ShapeDtypeStruct((ff, band), F32),
        jax.ShapeDtypeStruct((ff, band), F32),
    )
    results = pl.pallas_call(
        functools.partial(kernel, nz, ny),
        out_shape=shapes,
        in_specs=[hbm] * 7,
        out_specs=(vmem,) * 5,
        scratch_shapes=[
            pltpu.VMEM((1, toks), jnp.int32),
            pltpu.VMEM((1, toks), F32),
            pltpu.VMEM((3 * ff, width), BF),
            pltpu.VMEM((toks, quarter), BF),
            pltpu.VMEM((toks, quarter), BF),
            pltpu.VMEM((nz, ROWS, wide), BF),
            pltpu.VMEM((4, nz, ROWS, wide), BF),
            pltpu.VMEM((ny, 2, m, band), BF),
            pltpu.VMEM((ny, 2, m, band), BF),
            pltpu.VMEM((ny, m, band), BF),
            pltpu.VMEM((ny, m, band), BF),
            pltpu.VMEM((3 * ff, m), BF),
            pltpu.VMEM((3 * ff, m), BF),
            pltpu.VMEM((ny, 3 * ff, band), F32),
            pltpu.VMEM((ny, 3 * ff, band), BF),
            pltpu.VMEM((hy, 3 * ff, band), BF),
            pltpu.VMEM((hy, 3 * ff, band), BF),
            pltpu.VMEM((4, m, quarter), BF),
            pltpu.VMEM((2, m, quarter), BF),
            pltpu.VMEM((m, quarter), BF),
            pltpu.VMEM((m, quarter), BF),
            pltpu.VMEM((4, nz, LANES), F32),
            pltpu.VMEM((nz, ROWS, 3 * LANES), BF),
            pltpu.VMEM((nz, ROWS, 3 * LANES), BF),
            dma((9,)),
            dma((nz,)), dma((nz,)),
            dma((3, nz)), dma((3, nz)),
            dma((3,)), dma((3,)),
            dma((4,)), dma((4,)),
            dma((2, 2, 3)), dma((2, 2, 3)),
            dma((2, hy + 1, 4)), dma((2, hy + 1, 4)),
            dma((nz,)), dma((nz,)),
        ],
        compiler_params=pltpu.CompilerParams(
            collective_id=0, has_side_effects=True, vmem_limit_bytes=(53 * 1024 + 384) * 1024
        ),
    )(
        tokens, cotangent,
        expert_ids.reshape(1, toks), gate_probs.reshape(1, toks),
        w_gate[0].T, w_up[0].T, w_down[0],
    )
    anywhere = pl.BlockSpec(memory_space=pl.ANY)
    token_grad, prob_grad, grad_gate, grad_up, grad_down = pl.pallas_call(
        publish,
        out_shape=shapes,
        in_specs=[anywhere] * 5,
        out_specs=(anywhere,) * 5,
        scratch_shapes=[dma((5,))],
    )(*results)
    return (
        token_grad, prob_grad.reshape(toks, 1),
        grad_gate.T[None], grad_up.T[None], grad_down[None],
    )


def solution(mesh):
    rows = P(("island", "ep"), None)
    in_specs = (rows, rows, rows, rows, P("ep", None, "tp"), P("ep", None, "tp"), P("ep", "tp", None))
    out_specs = (
        P(("island", "ep"), "tp"), rows,
        P("ep", "island", "tp"), P("ep", "island", "tp"), P("ep", "tp", "island"),
    )
    return jax.shard_map(shards, mesh=mesh, in_specs=in_specs, out_specs=out_specs, check_vma=False)
```

```python
import functools

import jax
import jax.numpy as jnp
from jax import lax
from jax.experimental import pallas as pl
from jax.experimental.pallas import tpu as pltpu
from jax.sharding import PartitionSpec as P

CAP = 10
ROWS = 16
SPARE = ROWS - CAP
LANES = 128
TAIL = 4 * LANES
BF = jnp.bfloat16
F32 = jnp.float32
MESH = pl.DeviceIdType.MESH
NT = ((1,), (1,))


def dot(a, b, dims=((1,), (0,)), precision=None):
    return lax.dot_general(
        a, b, (dims, ((), ())), preferred_element_type=F32, precision=precision
    )


def iota(shape, dim):
    return lax.broadcasted_iota(jnp.int32, shape, dim)


def hot(condition):
    return jnp.where(condition, 1.0, 0.0).astype(BF)


def hops(nz):
    near = [1, 2] if nz > 8 else []
    pairs = []
    for d in range(nz // 2 - 1, len(near), -1):
        pairs += [d] + near[len(pairs) // 2 : len(pairs) // 2 + 1]
    return [nz // 2] + [d for pair in pairs for d in (pair, nz - pair)]


def kernel(
    nz, ny,
    tok, cot, ids_ref, probs_ref, wg, wu, wd,
    tg_ref, pg_ref, gg_ref, gu_ref, gd_ref,
    w, tq, cq, sb, rb, xs, ds, mx, md, gt, mgt, ch, cs, yl, yr, ip, xq, pk, rs, rr,
    ld, zs, zr, fs, fr, ms, mr, ps, pr, hs, hr, ys, yrs, vs, vr,
):
    t, z, island = lax.axis_index("tp"), lax.axis_index("ep"), lax.axis_index("island")
    y = lax.div(island, 2)
    core = island - 2 * y
    toks, quarter = tq.shape
    ff = wg.shape[0]
    m = nz * CAP
    n = nz * ROWS
    half = m // 2
    band = xs.shape[3]
    pairs = xs.shape[0]
    hz, hy = nz // 2, ny // 2
    piece_rows = 3 * ff // 4

    def tp_at(r):
        return {"tp": lax.rem(t + r, 4)}

    def ep_at(d):
        return {"ep": lax.rem(z + d, nz)}

    def y_at(d):
        return {"island": 2 * lax.rem(y + d, ny) + core}

    mate = {"island": 2 * y + 1 - core}

    def remote(src, dst, ssem, rsem, device):
        return pltpu.make_async_remote_copy(
            src_ref=src, dst_ref=dst, send_sem=ssem, recv_sem=rsem,
            device_id=device, device_id_type=MESH,
        )

    loads = [
        pltpu.make_async_copy(tok.at[:, pl.ds(pl.multiple_of(t * quarter, quarter), quarter)], tq, ld.at[0]),
        pltpu.make_async_copy(cot.at[:, pl.ds(pl.multiple_of(t * quarter, quarter), quarter)], cq, ld.at[1]),
        pltpu.make_async_copy(wg, w.at[pl.ds(0, ff)], ld.at[2]),
        pltpu.make_async_copy(wu, w.at[pl.ds(ff, ff)], ld.at[3]),
        pltpu.make_async_copy(wd, w.at[pl.ds(2 * ff, ff)], ld.at[4]),
    ]
    for copy in loads:
        copy.start()

    barrier = pltpu.get_barrier_semaphore()
    peers = [ep_at(d) for d in range(1, nz)] + [tp_at(r) for r in (1, 2, 3)]
    peers += [y_at(1), y_at(ny - 1), mate]
    for peer in peers:
        pl.semaphore_signal(barrier, inc=1, device_id=peer, device_id_type=MESH)

    ids = ids_ref[...]
    probs = probs_ref[...]
    named = hot(iota((nz, toks), 0) == ids)
    earlier = hot(iota((toks, toks), 0) < iota((toks, toks), 1))
    rank = jnp.sum(named.astype(F32) * dot(named, earlier), 0, keepdims=True)
    eye = iota((toks, toks), 0) == iota((toks, toks), 1)

    def column(row):
        return jnp.sum(jnp.where(eye, row, 0.0), 1, keepdims=True)

    probs_col = column(probs)
    ids_col = column(ids.astype(F32)).astype(jnp.int32)
    rank_col = column(rank).astype(jnp.int32)
    rank = rank.astype(jnp.int32)

    place = iota((n, toks), 0)
    block, row = lax.shift_right_logical(place, 4), place & (ROWS - 1)
    mine = block == ids
    pick_x = hot(mine & (row == rank))
    pick_d = hot(mine & (row == rank + CAP))
    piece = lax.shift_right_logical(row, 2)
    late = mine & ((row & 3) + SPARE == rank)
    pick_tail = [hot(late & (piece == c)) for c in range(4)]

    loads[0].wait()
    loads[1].wait()
    own_x = tq[...]
    own_d = (cq[...].astype(F32) * probs_col).astype(BF)
    main = dot(jnp.concatenate([pick_x, pick_d], 1), jnp.concatenate([own_x, own_d], 0))
    tail = dot(
        jnp.concatenate(pick_tail, 1),
        jnp.concatenate([own_d[:, LANES * c : LANES * (c + 1)] for c in range(4)], 0),
    )
    sb[:, :, 0:quarter] = main.astype(BF).reshape(nz, ROWS, quarter)
    sb[:, :, quarter : quarter + LANES] = tail.astype(BF).reshape(nz, ROWS, LANES)

    pl.semaphore_wait(barrier, len(peers))

    order = hops(nz)

    def z_copy(k):
        d = order[k]
        return remote(sb.at[lax.rem(z + d, nz)], rb.at[t, k + 1], zs.at[k], zr.at[k], ep_at(d))

    z_copies = [z_copy(k) for k in range(nz - 1)]
    own_block = pltpu.make_async_copy(sb.at[z], rb.at[t, 0], ld.at[5])
    own_block.start()
    for copy in z_copies:
        copy.start()

    left_q, right_q, far_q = lax.rem(t + 3, 4), lax.rem(t + 1, 4), lax.rem(t + 2, 4)

    def pass_right(p):
        return remote(rb.at[t, p], rb.at[t, p], fs.at[0, p], fr.at[0, p], tp_at(1))

    def pass_left(p):
        return remote(rb.at[t, p], rb.at[t, p], fs.at[1, p], fr.at[1, p], tp_at(3))

    def from_left(p):
        return remote(rb.at[t, p], rb.at[left_q, p], fs.at[0, p], fr.at[0, p], tp_at(1))

    def from_right(p):
        return remote(rb.at[t, p], rb.at[right_q, p], fs.at[1, p], fr.at[1, p], tp_at(3))

    direct = nz - 4 if nz > 8 else nz // 2

    def onward(p):
        if p >= direct:
            return remote(rb.at[t, p], rb.at[t, p], fs.at[2, p], fr.at[2, p], tp_at(2))
        q, to = (right_q, 3) if p % 2 else (left_q, 1)
        return remote(rb.at[q, p], rb.at[q, p], fs.at[2, p], fr.at[2, p], tp_at(to))

    def from_far(p):
        return remote(rb.at[t, p], rb.at[far_q, p], fs.at[2, p], fr.at[2, p], tp_at(1))

    def relay(p):
        from_left(p).wait_recv()
        from_right(p).wait_recv()
        onward(p).start()

    behind = 4
    for p in range(nz):
        if p == 0:
            own_block.wait()
        else:
            z_copies[p - 1].wait_recv()
        if p >= direct:
            onward(p).start()
        pass_right(p).start()
        pass_left(p).start()
        if 0 <= p - behind < direct:
            relay(p - behind)
    for p in range(max(0, nz - behind), direct):
        relay(p)

    rows = iota((half, n // 2), 0)
    source = lax.shift_right_logical(rows * 6554, 16)
    slot = rows - CAP * source
    there = iota((half, n // 2), 1)
    unpick_x = hot(there == ROWS * source + slot)
    unpick_d = hot((slot < SPARE) & (there == ROWS * source + CAP + slot))
    unpick_tail = [
        hot((slot >= SPARE) & (there == ROWS * source + 4 * c + slot - SPARE)) for c in range(4)
    ]
    unpick_main = jnp.concatenate([unpick_x, unpick_d], 0)
    unpick_tail = jnp.concatenate(unpick_tail, 0)
    per = quarter // band
    for g in range(2):
        for p in range(g * hz, g * hz + hz):
            if p >= direct:
                from_left(p).wait_recv()
                from_right(p).wait_recv()
            from_far(p).wait_recv()
        here = pl.ds(g * half, half)
        for q in range(4):
            got = rb[q, pl.ds(g * hz, hz)].reshape(n // 2, quarter + LANES)
            both = dot(unpick_main, got[:, 0:quarter])
            ends = dot(unpick_tail, got[:, quarter : quarter + LANES])
            ends = jnp.concatenate([ends[half * c : half * (c + 1)] for c in range(4)], 1)
            x_rows = both[0:half].astype(BF)
            d_rows = (both[half : 2 * half] + ends).astype(BF)
            for b in range(per):
                at = q * per + b
                xs[at // 2, at % 2, here, :] = x_rows[:, band * b : band * (b + 1)]
                ds[at // 2, at % 2, here, :] = d_rows[:, band * b : band * (b + 1)]

    mate_x = remote(xs.at[:, 1 - core], mx, ms.at[0], mr.at[0], mate)
    mate_d = remote(ds.at[:, 1 - core], md, ms.at[1], mr.at[1], mate)
    mate_g = remote(gt, mgt, ms.at[2], mr.at[2], mate)
    mate_x.start()
    mate_d.start()

    for copy in loads[2:]:
        copy.wait()
    x_all = jnp.concatenate([xs[o, c] for o in range(pairs) for c in range(2)], 1)
    d_all = jnp.concatenate([ds[o, c] for o in range(pairs) for c in range(2)], 1)
    gate_up = dot(w[0 : 2 * ff, :], x_all, NT)
    back = dot(w[2 * ff : 3 * ff, :], d_all, NT)
    gate, up = gate_up[0:ff], gate_up[ff : 2 * ff]
    sigma = jax.nn.sigmoid(gate)
    active = gate * sigma
    hidden = (active * up).astype(BF)
    gt[0:ff, :] = (back * up * sigma * (1.0 + gate * (1.0 - sigma))).astype(BF)
    gt[ff : 2 * ff, :] = (back * active).astype(BF)
    gt[2 * ff : 3 * ff, :] = hidden
    mate_g.start()

    eye_m = hot(iota((m, m), 0) == iota((m, m), 1))
    d_rows = dot(eye_m, gt[0 : 2 * ff, :], NT).astype(BF)

    def input_part(r):
        q = lax.rem(t + r, 4)
        cols = pl.ds(pl.multiple_of(q * quarter, quarter), quarter)
        ip[r] = dot(d_rows, w[0 : 2 * ff, cols]).astype(BF)

    def tp_copy(g, r):
        here = pl.ds(g * half, half)
        return remote(ip.at[r, here], xq.at[r - 1, here], hs.at[g, r], hr.at[g, r], tp_at(r))

    tp_copies = [[tp_copy(g, r) for r in (1, 2, 3)] for g in range(2)]

    def weight_part(*js):
        def cat(blocks):
            return blocks[0] if len(blocks) == 1 else jnp.concatenate(blocks, 1)

        os = [lax.rem(y + j, ny) for j in js]
        top = dot(gt[0 : 2 * ff, :], cat([xs[o, core] for o in os]))
        top = top + dot(mgt[0 : 2 * ff, :], cat([mx[o] for o in os]))
        low = dot(gt[2 * ff : 3 * ff, :], cat([ds[o, core] for o in os]))
        low = low + dot(mgt[2 * ff : 3 * ff, :], cat([md[o] for o in os]))
        for i, j in enumerate(js):
            ch[j, 0 : 2 * ff, :] = top[:, band * i : band * (i + 1)]
            ch[j, 2 * ff : 3 * ff, :] = low[:, band * i : band * (i + 1)]

    def y_copy(side, dist, part):
        j = dist if side == 0 else ny - dist
        where = pl.ds(part * piece_rows, piece_rows)
        into = (yl, yr)[side]
        return remote(
            cs.at[j, where], into.at[dist - 1, where],
            ys.at[side, dist, part], yrs.at[side, dist, part], y_at(1 if side == 0 else ny - 1),
        )

    far_parts, near_parts = ((0, 1), (2, 3)), ((2, 3), (0, 1))

    def y_step(side, dist, part):
        j = dist if side == 0 else ny - dist
        where = pl.ds(part * piece_rows, piece_rows)
        if dist == hy or (dist == hy - 1 and part in near_parts[side]):
            cs[j, where, :] = ch[j, where, :].astype(BF)
        else:
            y_copy(side, dist + 1, part).wait_recv()
            came = (yl, yr)[side][dist, where, :].astype(F32)
            cs[j, where, :] = (ch[j, where, :] + came).astype(BF)
        y_copy(side, dist, part).start()

    def y_steps(dist, parts):
        for i in range(2):
            for side in (0, 1):
                y_step(side, dist, parts[side][i])

    for r in (2, 1, 3):
        input_part(r)
        tp_copies[0][r - 1].start()
    for r in (2, 1, 3):
        tp_copies[1][r - 1].start()

    mate_x.wait_recv()
    mate_d.wait_recv()
    mate_g.wait_recv()
    weight_part(hy)
    y_steps(hy, far_parts)
    weight_part(hy - 1, ny - hy + 1)
    y_steps(hy - 1, near_parts)

    prob_row = jnp.sum(hidden.astype(F32) * back, 0, keepdims=True)
    in_source = iota((nz, m), 0) == lax.shift_right_logical(iota((nz, m), 1) * 6554, 16)
    at_row = iota((m, LANES), 0)
    at_slot = iota((m, LANES), 1) == at_row - CAP * lax.shift_right_logical(at_row * 6554, 16)
    pk[0] = dot(
        jnp.where(in_source, prob_row, 0.0), jnp.where(at_slot, 1.0, 0.0),
        precision=lax.Precision.HIGHEST,
    )
    prob_sends = [remote(pk.at[0], pk.at[r], ps.at[r], pr.at[r], tp_at(r)) for r in (1, 2, 3)]
    for copy in prob_sends:
        copy.start()
    input_part(0)
    y_steps(hy - 1, far_parts)
    for dist in range(hy - 2, 0, -1):
        weight_part(dist, ny - dist)

    for copy in prob_sends:
        copy.wait_recv()
    prob = (pk[0] + pk[1]) + (pk[2] + pk[3])
    prob_high = prob.astype(BF)
    prob_low = (prob - prob_high.astype(F32)).astype(BF)
    to = iota((n // 2, half), 0)
    block, row = lax.shift_right_logical(to, 4), to & (ROWS - 1)
    first = CAP * block
    frm = iota((n // 2, half), 1)
    pack = hot((row < CAP) & (frm == first + row))
    pack_0 = hot((row >= CAP) & (frm == first + row - CAP))
    pack_1 = hot((row >= CAP) & (row < ROWS - 2) & (frm == first + row - CAP + SPARE))
    to = iota((n // 2, nz), 0)
    block, row = lax.shift_right_logical(to, 4), to & (ROWS - 1)

    def back_copy(k):
        d = nz - order[k]
        return remote(rs.at[k + 1], rr.at[z], vs.at[k], vr.at[k], ep_at(d))

    def back_recv(k):
        return remote(rs.at[0], rr.at[lax.rem(z + order[k], nz)], vs.at[k], vr.at[k], ep_at(1))

    def send_back(g):
        for copy in tp_copies[g]:
            copy.wait_recv()
        here = pl.ds(g * half, half)
        summed = ip[0, here, :].astype(F32) + xq[0, here, :].astype(F32)
        summed = summed + (xq[1, here, :].astype(F32) + xq[2, here, :].astype(F32))
        summed = summed.astype(BF)
        ends = summed[:, 3 * LANES : 4 * LANES]
        same = block + g * hz == iota((n // 2, nz), 1)
        extra = dot(hot(same & (row == CAP)), prob_high) + dot(hot(same & (row == CAP + 1)), prob_low)
        packed = dot(pack, summed[:, 0 : 3 * LANES])
        packed = packed + jnp.concatenate([dot(pack_0, ends), dot(pack_1, ends), extra], 1)
        rs[pl.ds(g * hz, hz)] = packed.astype(BF).reshape(hz, ROWS, 3 * LANES)
        for k in range(max(g * hz - 1, 0), g * hz + hz - 1):
            back_copy(k).start()

    send_back(0)
    if hy > 2:
        y_steps(hy - 2, near_parts)
    send_back(1)
    own_back = pltpu.make_async_copy(rs.at[0], rr.at[z], ld.at[6])
    own_back.start()
    for dist in range(hy - 2, 0, -1):
        if dist < hy - 2:
            y_steps(dist, near_parts)
        y_steps(dist, far_parts)
    weight_part(0)
    for parts_at in (near_parts, far_parts):
        for i in range(2):
            for side in (0, 1):
                y_copy(side, 1, parts_at[side][i]).wait_recv()
    total = ch[0] + (yl[0].astype(F32) + yr[0].astype(F32))
    gg_ref[...] = total[0:ff]
    gu_ref[...] = total[ff : 2 * ff]
    gd_ref[...] = total[2 * ff : 3 * ff]

    at = iota((toks, n), 1)
    block, row = lax.shift_right_logical(at, 4), at & (ROWS - 1)
    mine = block == ids_col
    take = hot(mine & (row == rank_col))
    take_0 = hot(mine & (row == rank_col + CAP) & (rank_col < SPARE))
    take_1 = hot(mine & (row == rank_col + CAP - SPARE) & (rank_col >= SPARE))
    take_high, take_low = hot(mine & (row == CAP)), hot(mine & (row == CAP + 1))

    for k in range(nz - 1):
        back_recv(k).wait_recv()
    own_back.wait()
    got = rr[...].reshape(n, 3 * LANES)
    tg_ref[:, 0 : 3 * LANES] = dot(take, got).astype(BF)
    tg_ref[:, 3 * LANES : 4 * LANES] = (
        dot(take_0, got[:, 0:LANES]) + dot(take_1, got[:, LANES : 2 * LANES])
    ).astype(BF)
    ends = got[:, 2 * LANES : 3 * LANES]
    chosen = iota((toks, LANES), 1) == rank_col
    value = jnp.where(chosen, dot(take_high, ends) + dot(take_low, ends), 0.0)
    value = jnp.sum(value, 1, keepdims=True) / probs_col
    pg_ref[...] = jnp.sum(jnp.where(eye, value, 0.0), 0, keepdims=True)

    for k in range(nz - 1):
        z_copies[k].wait_send()
        back_copy(k).wait_send()
    for p in range(nz):
        pass_right(p).wait_send()
        pass_left(p).wait_send()
        onward(p).wait_send()
    for copy in [mate_x, mate_d, mate_g] + prob_sends:
        copy.wait_send()
    for copy in tp_copies[0] + tp_copies[1]:
        copy.wait_send()
    for side in (0, 1):
        for part in far_parts[side]:
            y_copy(side, hy, part).wait_send()
        for dist in range(hy - 1, 0, -1):
            for part in range(4):
                y_copy(side, dist, part).wait_send()


def publish(*refs):
    copies = [pltpu.make_async_copy(refs[i], refs[i + 5], refs[10].at[i]) for i in range(5)]
    for copy in copies:
        copy.start()
    for copy in copies:
        copy.wait()


def shards(tokens, cotangent, expert_ids, gate_probs, w_gate, w_up, w_down):
    toks, width = tokens.shape
    ff = w_down.shape[1]
    nz, ny = lax.axis_size("ep"), lax.axis_size("island") // 2
    quarter, band = width // 4, width // (2 * ny)
    m = nz * CAP
    wide = quarter + LANES
    hy, hz = ny // 2, nz // 2
    hbm = pl.BlockSpec(memory_space=pltpu.HBM)
    vmem = pl.BlockSpec(memory_space=pltpu.VMEM)
    dma = pltpu.SemaphoreType.DMA
    shapes = (
        jax.ShapeDtypeStruct((toks, quarter), BF),
        jax.ShapeDtypeStruct((1, toks), F32),
        jax.ShapeDtypeStruct((ff, band), F32),
        jax.ShapeDtypeStruct((ff, band), F32),
        jax.ShapeDtypeStruct((ff, band), F32),
    )
    results = pl.pallas_call(
        functools.partial(kernel, nz, ny),
        out_shape=shapes,
        in_specs=[hbm, hbm, vmem, vmem, hbm, hbm, hbm],
        out_specs=(vmem,) * 5,
        scratch_shapes=[
            pltpu.VMEM((3 * ff, width), BF),
            pltpu.VMEM((toks, quarter), BF),
            pltpu.VMEM((toks, quarter), BF),
            pltpu.VMEM((nz, ROWS, wide), BF),
            pltpu.VMEM((4, nz, ROWS, wide), BF),
            pltpu.VMEM((ny, 2, m, band), BF),
            pltpu.VMEM((ny, 2, m, band), BF),
            pltpu.VMEM((ny, m, band), BF),
            pltpu.VMEM((ny, m, band), BF),
            pltpu.VMEM((3 * ff, m), BF),
            pltpu.VMEM((3 * ff, m), BF),
            pltpu.VMEM((ny, 3 * ff, band), F32),
            pltpu.VMEM((ny, 3 * ff, band), BF),
            pltpu.VMEM((hy, 3 * ff, band), BF),
            pltpu.VMEM((hy, 3 * ff, band), BF),
            pltpu.VMEM((4, m, quarter), BF),
            pltpu.VMEM((3, m, quarter), BF),
            pltpu.VMEM((4, nz, LANES), F32),
            pltpu.VMEM((nz, ROWS, 3 * LANES), BF),
            pltpu.VMEM((nz, ROWS, 3 * LANES), BF),
            dma((7,)),
            dma((nz,)), dma((nz,)),
            dma((3, nz)), dma((3, nz)),
            dma((3,)), dma((3,)),
            dma((4,)), dma((4,)),
            dma((2, 4)), dma((2, 4)),
            dma((2, hy + 1, 4)), dma((2, hy + 1, 4)),
            dma((nz,)), dma((nz,)),
        ],
        compiler_params=pltpu.CompilerParams(
            collective_id=0, has_side_effects=True, vmem_limit_bytes=(53 * 1024 + 384) * 1024
        ),
    )(
        tokens, cotangent,
        expert_ids.reshape(1, toks), gate_probs.reshape(1, toks),
        w_gate[0].T, w_up[0].T, w_down[0],
    )
    anywhere = pl.BlockSpec(memory_space=pl.ANY)
    token_grad, prob_grad, grad_gate, grad_up, grad_down = pl.pallas_call(
        publish,
        out_shape=shapes,
        in_specs=[anywhere] * 5,
        out_specs=(anywhere,) * 5,
        scratch_shapes=[dma((5,))],
        compiler_params=pltpu.CompilerParams(vmem_limit_bytes=4 * 1024 * 1024),
    )(*results)
    return (
        token_grad, prob_grad.reshape(toks, 1),
        grad_gate.T[None], grad_up.T[None], grad_down[None],
    )


def solution(mesh):
    rows = P(("island", "ep"), None)
    in_specs = (rows, rows, rows, rows, P("ep", None, "tp"), P("ep", None, "tp"), P("ep", "tp", None))
    out_specs = (
        P(("island", "ep"), "tp"), rows,
        P("ep", "island", "tp"), P("ep", "island", "tp"), P("ep", "tp", "island"),
    )
    return jax.shard_map(shards, mesh=mesh, in_specs=in_specs, out_specs=out_specs, check_vma=False)
```

```python
import functools

import jax
import jax.numpy as jnp
from jax import lax
from jax.experimental import pallas as pl
from jax.experimental.pallas import tpu as pltpu
from jax.sharding import PartitionSpec as P

CAP = 10
ROWS = 16
SPARE = ROWS - CAP
LANES = 128
TAIL = 4 * LANES
BF = jnp.bfloat16
F32 = jnp.float32
MESH = pl.DeviceIdType.MESH
NT = ((1,), (1,))


def dot(a, b, dims=((1,), (0,)), precision=None):
    return lax.dot_general(
        a, b, (dims, ((), ())), preferred_element_type=F32, precision=precision
    )


def iota(shape, dim):
    return lax.broadcasted_iota(jnp.int32, shape, dim)


def hot(condition):
    return jnp.where(condition, 1.0, 0.0).astype(BF)


def hops(nz):
    near = [1, 2] if nz > 8 else []
    pairs = []
    for d in range(nz // 2 - 1, len(near), -1):
        pairs += [d] + near[len(pairs) // 2 : len(pairs) // 2 + 1]
    return [nz // 2] + [d for pair in pairs for d in (pair, nz - pair)]


def kernel(
    nz, ny,
    tok, cot, ids_ref, probs_ref, wg, wu, wd,
    tg_ref, pg_ref, gg_ref, gu_ref, gd_ref,
    w, tq, cq, sb, rb, xs, ds, mx, md, gt, mgt, ch, cs, yl, yr, ip, xq, pk, rs, rr,
    ld, zs, zr, fs, fr, ms, mr, ps, pr, hs, hr, ys, yrs, vs, vr,
):
    t, z, island = lax.axis_index("tp"), lax.axis_index("ep"), lax.axis_index("island")
    y = lax.div(island, 2)
    core = island - 2 * y
    toks, quarter = tq.shape
    ff = wg.shape[0]
    m = nz * CAP
    n = nz * ROWS
    half = m // 2
    band = xs.shape[3]
    pairs = xs.shape[0]
    hz, hy = nz // 2, ny // 2
    piece_rows = 3 * ff // 4

    def tp_at(r):
        return {"tp": lax.rem(t + r, 4)}

    def ep_at(d):
        return {"ep": lax.rem(z + d, nz)}

    def y_at(d):
        return {"island": 2 * lax.rem(y + d, ny) + core}

    mate = {"island": 2 * y + 1 - core}

    def remote(src, dst, ssem, rsem, device):
        return pltpu.make_async_remote_copy(
            src_ref=src, dst_ref=dst, send_sem=ssem, recv_sem=rsem,
            device_id=device, device_id_type=MESH,
        )

    loads = [
        pltpu.make_async_copy(tok.at[:, pl.ds(pl.multiple_of(t * quarter, quarter), quarter)], tq, ld.at[0]),
        pltpu.make_async_copy(cot.at[:, pl.ds(pl.multiple_of(t * quarter, quarter), quarter)], cq, ld.at[1]),
        pltpu.make_async_copy(wg, w.at[pl.ds(0, ff)], ld.at[2]),
        pltpu.make_async_copy(wu, w.at[pl.ds(ff, ff)], ld.at[3]),
        pltpu.make_async_copy(wd, w.at[pl.ds(2 * ff, ff)], ld.at[4]),
    ]
    for copy in loads:
        copy.start()

    barrier = pltpu.get_barrier_semaphore()
    peers = [ep_at(d) for d in range(1, nz)] + [tp_at(r) for r in (1, 2, 3)]
    peers += [y_at(1), y_at(ny - 1), mate]
    for peer in peers:
        pl.semaphore_signal(barrier, inc=1, device_id=peer, device_id_type=MESH)

    ids = ids_ref[...]
    probs = probs_ref[...]
    named = hot(iota((nz, toks), 0) == ids)
    earlier = hot(iota((toks, toks), 0) < iota((toks, toks), 1))
    rank = jnp.sum(named.astype(F32) * dot(named, earlier), 0, keepdims=True)
    eye = iota((toks, toks), 0) == iota((toks, toks), 1)

    def column(row):
        return jnp.sum(jnp.where(eye, row, 0.0), 1, keepdims=True)

    probs_col = column(probs)
    ids_col = column(ids.astype(F32)).astype(jnp.int32)
    rank_col = column(rank).astype(jnp.int32)
    rank = rank.astype(jnp.int32)

    place = iota((n, toks), 0)
    block, row = lax.shift_right_logical(place, 4), place & (ROWS - 1)
    mine = block == ids
    pick_x = hot(mine & (row == rank))
    pick_d = hot(mine & (row == rank + CAP))
    piece = lax.shift_right_logical(row, 2)
    late = mine & ((row & 3) + SPARE == rank)
    pick_tail = [hot(late & (piece == c)) for c in range(4)]

    loads[0].wait()
    loads[1].wait()
    own_x = tq[...]
    own_d = (cq[...].astype(F32) * probs_col).astype(BF)
    main = dot(jnp.concatenate([pick_x, pick_d], 1), jnp.concatenate([own_x, own_d], 0))
    tail = dot(
        jnp.concatenate(pick_tail, 1),
        jnp.concatenate([own_d[:, LANES * c : LANES * (c + 1)] for c in range(4)], 0),
    )
    sb[:, :, 0:quarter] = main.astype(BF).reshape(nz, ROWS, quarter)
    sb[:, :, quarter : quarter + LANES] = tail.astype(BF).reshape(nz, ROWS, LANES)

    pl.semaphore_wait(barrier, len(peers))

    order = hops(nz)

    def z_copy(k):
        d = order[k]
        return remote(sb.at[lax.rem(z + d, nz)], rb.at[t, k + 1], zs.at[k], zr.at[k], ep_at(d))

    z_copies = [z_copy(k) for k in range(nz - 1)]
    own_block = pltpu.make_async_copy(sb.at[z], rb.at[t, 0], ld.at[5])
    own_block.start()
    ahead = 6
    for copy in z_copies[:ahead]:
        copy.start()

    left_q, right_q, far_q = lax.rem(t + 3, 4), lax.rem(t + 1, 4), lax.rem(t + 2, 4)

    def pass_right(p):
        return remote(rb.at[t, p], rb.at[t, p], fs.at[0, p], fr.at[0, p], tp_at(1))

    def pass_left(p):
        return remote(rb.at[t, p], rb.at[t, p], fs.at[1, p], fr.at[1, p], tp_at(3))

    def from_left(p):
        return remote(rb.at[t, p], rb.at[left_q, p], fs.at[0, p], fr.at[0, p], tp_at(1))

    def from_right(p):
        return remote(rb.at[t, p], rb.at[right_q, p], fs.at[1, p], fr.at[1, p], tp_at(3))

    direct = nz - 4 if nz > 8 else nz // 2

    def onward(p):
        if p >= direct:
            return remote(rb.at[t, p], rb.at[t, p], fs.at[2, p], fr.at[2, p], tp_at(2))
        q, to = (right_q, 3) if p % 2 else (left_q, 1)
        return remote(rb.at[q, p], rb.at[q, p], fs.at[2, p], fr.at[2, p], tp_at(to))

    def from_far(p):
        return remote(rb.at[t, p], rb.at[far_q, p], fs.at[2, p], fr.at[2, p], tp_at(1))

    def relay(p):
        from_left(p).wait_recv()
        from_right(p).wait_recv()
        onward(p).start()

    behind = 4
    for p in range(nz):
        if p == 0:
            own_block.wait()
        else:
            z_copies[p - 1].wait_recv()
            for copy in z_copies[p - 1 + ahead : p + ahead]:
                copy.start()
        if p >= direct:
            onward(p).start()
        pass_right(p).start()
        pass_left(p).start()
        if 0 <= p - behind < direct:
            relay(p - behind)
    for p in range(max(0, nz - behind), direct):
        relay(p)

    rows = iota((half, n // 2), 0)
    source = lax.shift_right_logical(rows * 6554, 16)
    slot = rows - CAP * source
    there = iota((half, n // 2), 1)
    unpick_x = hot(there == ROWS * source + slot)
    unpick_d = hot((slot < SPARE) & (there == ROWS * source + CAP + slot))
    unpick_tail = [
        hot((slot >= SPARE) & (there == ROWS * source + 4 * c + slot - SPARE)) for c in range(4)
    ]
    unpick_main = jnp.concatenate([unpick_x, unpick_d], 0)
    unpick_tail = jnp.concatenate(unpick_tail, 0)
    per = quarter // band
    for g in range(2):
        for p in range(g * hz, g * hz + hz):
            if p >= direct:
                from_left(p).wait_recv()
                from_right(p).wait_recv()
            from_far(p).wait_recv()
        here = pl.ds(g * half, half)
        for q in range(4):
            got = rb[q, pl.ds(g * hz, hz)].reshape(n // 2, quarter + LANES)
            both = dot(unpick_main, got[:, 0:quarter])
            ends = dot(unpick_tail, got[:, quarter : quarter + LANES])
            ends = jnp.concatenate([ends[half * c : half * (c + 1)] for c in range(4)], 1)
            x_rows = both[0:half].astype(BF)
            d_rows = (both[half : 2 * half] + ends).astype(BF)
            for b in range(per):
                at = q * per + b
                xs[at // 2, at % 2, here, :] = x_rows[:, band * b : band * (b + 1)]
                ds[at // 2, at % 2, here, :] = d_rows[:, band * b : band * (b + 1)]

    mate_x = remote(xs.at[:, 1 - core], mx, ms.at[0], mr.at[0], mate)
    mate_d = remote(ds.at[:, 1 - core], md, ms.at[1], mr.at[1], mate)
    mate_g = remote(gt, mgt, ms.at[2], mr.at[2], mate)
    mate_x.start()
    mate_d.start()

    for copy in loads[2:]:
        copy.wait()
    x_all = jnp.concatenate([xs[o, c] for o in range(pairs) for c in range(2)], 1)
    d_all = jnp.concatenate([ds[o, c] for o in range(pairs) for c in range(2)], 1)
    gate_up = dot(w[0 : 2 * ff, :], x_all, NT)
    back = dot(w[2 * ff : 3 * ff, :], d_all, NT)
    gate, up = gate_up[0:ff], gate_up[ff : 2 * ff]
    sigma = jax.nn.sigmoid(gate)
    active = gate * sigma
    hidden = (active * up).astype(BF)
    gt[0:ff, :] = (back * up * sigma * (1.0 + gate * (1.0 - sigma))).astype(BF)
    gt[ff : 2 * ff, :] = (back * active).astype(BF)
    gt[2 * ff : 3 * ff, :] = hidden
    mate_g.start()

    eye_m = hot(iota((m, m), 0) == iota((m, m), 1))
    d_rows = dot(eye_m, gt[0 : 2 * ff, :], NT).astype(BF)

    def input_part(r):
        q = lax.rem(t + r, 4)
        cols = pl.ds(pl.multiple_of(q * quarter, quarter), quarter)
        ip[r] = dot(d_rows, w[0 : 2 * ff, cols]).astype(BF)

    def tp_copy(g, r):
        here = pl.ds(g * half, half)
        return remote(ip.at[r, here], xq.at[r - 1, here], hs.at[g, r], hr.at[g, r], tp_at(r))

    tp_copies = [[tp_copy(g, r) for r in (1, 2, 3)] for g in range(2)]

    def weight_part(*js):
        def cat(blocks):
            return blocks[0] if len(blocks) == 1 else jnp.concatenate(blocks, 1)

        os = [lax.rem(y + j, ny) for j in js]
        top = dot(gt[0 : 2 * ff, :], cat([xs[o, core] for o in os]))
        top = top + dot(mgt[0 : 2 * ff, :], cat([mx[o] for o in os]))
        low = dot(gt[2 * ff : 3 * ff, :], cat([ds[o, core] for o in os]))
        low = low + dot(mgt[2 * ff : 3 * ff, :], cat([md[o] for o in os]))
        for i, j in enumerate(js):
            ch[j, 0 : 2 * ff, :] = top[:, band * i : band * (i + 1)]
            ch[j, 2 * ff : 3 * ff, :] = low[:, band * i : band * (i + 1)]

    def y_copy(side, dist, part):
        j = dist if side == 0 else ny - dist
        where = pl.ds(part * piece_rows, piece_rows)
        into = (yl, yr)[side]
        return remote(
            cs.at[j, where], into.at[dist - 1, where],
            ys.at[side, dist, part], yrs.at[side, dist, part], y_at(1 if side == 0 else ny - 1),
        )

    far_parts, near_parts = ((0, 1), (2, 3)), ((2, 3), (0, 1))

    def y_step(side, dist, part):
        j = dist if side == 0 else ny - dist
        where = pl.ds(part * piece_rows, piece_rows)
        if dist == hy or (dist == hy - 1 and part in near_parts[side]):
            cs[j, where, :] = ch[j, where, :].astype(BF)
        else:
            y_copy(side, dist + 1, part).wait_recv()
            came = (yl, yr)[side][dist, where, :].astype(F32)
            cs[j, where, :] = (ch[j, where, :] + came).astype(BF)
        y_copy(side, dist, part).start()

    def y_steps(dist, parts):
        for i in range(2):
            for side in (0, 1):
                y_step(side, dist, parts[side][i])

    for r in (2, 1, 3):
        input_part(r)
        tp_copies[0][r - 1].start()
    for r in (2, 1, 3):
        tp_copies[1][r - 1].start()

    input_part(0)
    prob_row = jnp.sum(hidden.astype(F32) * back, 0, keepdims=True)
    in_source = iota((nz, m), 0) == lax.shift_right_logical(iota((nz, m), 1) * 6554, 16)
    at_row = iota((m, LANES), 0)
    at_slot = iota((m, LANES), 1) == at_row - CAP * lax.shift_right_logical(at_row * 6554, 16)
    pk[0] = dot(
        jnp.where(in_source, prob_row, 0.0), jnp.where(at_slot, 1.0, 0.0),
        precision=lax.Precision.HIGHEST,
    )
    prob_sends = [remote(pk.at[0], pk.at[r], ps.at[r], pr.at[r], tp_at(r)) for r in (1, 2, 3)]
    for copy in prob_sends:
        copy.start()

    mate_x.wait_recv()
    mate_d.wait_recv()
    mate_g.wait_recv()
    weight_part(hy)
    y_steps(hy, far_parts)
    weight_part(hy - 1, ny - hy + 1)
    y_steps(hy - 1, near_parts)
    if hy > 2:
        weight_part(hy - 2, ny - hy + 2)
    y_steps(hy - 1, far_parts)

    for copy in prob_sends:
        copy.wait_recv()
    prob = (pk[0] + pk[1]) + (pk[2] + pk[3])
    prob_high = prob.astype(BF)
    prob_low = (prob - prob_high.astype(F32)).astype(BF)
    to = iota((n // 2, half), 0)
    block, row = lax.shift_right_logical(to, 4), to & (ROWS - 1)
    first = CAP * block
    frm = iota((n // 2, half), 1)
    pack = hot((row < CAP) & (frm == first + row))
    pack_0 = hot((row >= CAP) & (frm == first + row - CAP))
    pack_1 = hot((row >= CAP) & (row < ROWS - 2) & (frm == first + row - CAP + SPARE))
    to = iota((n // 2, nz), 0)
    block, row = lax.shift_right_logical(to, 4), to & (ROWS - 1)

    def back_copy(k):
        d = nz - order[k]
        return remote(rs.at[k + 1], rr.at[z], vs.at[k], vr.at[k], ep_at(d))

    def back_recv(k):
        return remote(rs.at[0], rr.at[lax.rem(z + order[k], nz)], vs.at[k], vr.at[k], ep_at(1))

    def send_back(g):
        for copy in tp_copies[g]:
            copy.wait_recv()
        here = pl.ds(g * half, half)
        summed = ip[0, here, :].astype(F32) + xq[0, here, :].astype(F32)
        summed = summed + (xq[1, here, :].astype(F32) + xq[2, here, :].astype(F32))
        summed = summed.astype(BF)
        ends = summed[:, 3 * LANES : 4 * LANES]
        same = block + g * hz == iota((n // 2, nz), 1)
        extra = dot(hot(same & (row == CAP)), prob_high) + dot(hot(same & (row == CAP + 1)), prob_low)
        packed = dot(pack, summed[:, 0 : 3 * LANES])
        packed = packed + jnp.concatenate([dot(pack_0, ends), dot(pack_1, ends), extra], 1)
        rs[pl.ds(g * hz, hz)] = packed.astype(BF).reshape(hz, ROWS, 3 * LANES)
        for k in range(max(g * hz - 1, 0), g * hz + hz - 1):
            back_copy(k).start()

    send_back(0)
    own_back = pltpu.make_async_copy(rs.at[0], rr.at[z], ld.at[6])
    own_back.start()
    for dist in range(hy - 2, 0, -1):
        y_steps(dist, near_parts)
        if dist > 1:
            weight_part(dist - 1, ny - dist + 1)
            y_steps(dist, far_parts)
    send_back(1)
    if hy > 2:
        y_steps(1, far_parts)
    weight_part(0)
    for parts_at in (near_parts, far_parts):
        for i in range(2):
            for side in (0, 1):
                y_copy(side, 1, parts_at[side][i]).wait_recv()
    total = ch[0] + (yl[0].astype(F32) + yr[0].astype(F32))
    gg_ref[...] = total[0:ff]
    gu_ref[...] = total[ff : 2 * ff]
    gd_ref[...] = total[2 * ff : 3 * ff]

    at = iota((toks, n), 1)
    block, row = lax.shift_right_logical(at, 4), at & (ROWS - 1)
    mine = block == ids_col
    take = hot(mine & (row == rank_col))
    take_0 = hot(mine & (row == rank_col + CAP) & (rank_col < SPARE))
    take_1 = hot(mine & (row == rank_col + CAP - SPARE) & (rank_col >= SPARE))
    take_high, take_low = hot(mine & (row == CAP)), hot(mine & (row == CAP + 1))

    for k in range(nz - 1):
        back_recv(k).wait_recv()
    own_back.wait()
    got = rr[...].reshape(n, 3 * LANES)
    tg_ref[:, 0 : 3 * LANES] = dot(take, got).astype(BF)
    tg_ref[:, 3 * LANES : 4 * LANES] = (
        dot(take_0, got[:, 0:LANES]) + dot(take_1, got[:, LANES : 2 * LANES])
    ).astype(BF)
    ends = got[:, 2 * LANES : 3 * LANES]
    chosen = iota((toks, LANES), 1) == rank_col
    value = jnp.where(chosen, dot(take_high, ends) + dot(take_low, ends), 0.0)
    value = jnp.sum(value, 1, keepdims=True) / probs_col
    pg_ref[...] = jnp.sum(jnp.where(eye, value, 0.0), 0, keepdims=True)

    for k in range(nz - 1):
        z_copies[k].wait_send()
        back_copy(k).wait_send()
    for p in range(nz):
        pass_right(p).wait_send()
        pass_left(p).wait_send()
        onward(p).wait_send()
    for copy in [mate_x, mate_d, mate_g] + prob_sends:
        copy.wait_send()
    for copy in tp_copies[0] + tp_copies[1]:
        copy.wait_send()
    for side in (0, 1):
        for part in far_parts[side]:
            y_copy(side, hy, part).wait_send()
        for dist in range(hy - 1, 0, -1):
            for part in range(4):
                y_copy(side, dist, part).wait_send()


def publish(*refs):
    copies = [pltpu.make_async_copy(refs[i], refs[i + 5], refs[10].at[i]) for i in range(5)]
    for copy in copies:
        copy.start()
    for copy in copies:
        copy.wait()


def shards(tokens, cotangent, expert_ids, gate_probs, w_gate, w_up, w_down):
    toks, width = tokens.shape
    ff = w_down.shape[1]
    nz, ny = lax.axis_size("ep"), lax.axis_size("island") // 2
    quarter, band = width // 4, width // (2 * ny)
    m = nz * CAP
    wide = quarter + LANES
    hy, hz = ny // 2, nz // 2
    hbm = pl.BlockSpec(memory_space=pltpu.HBM)
    vmem = pl.BlockSpec(memory_space=pltpu.VMEM)
    dma = pltpu.SemaphoreType.DMA
    shapes = (
        jax.ShapeDtypeStruct((toks, quarter), BF),
        jax.ShapeDtypeStruct((1, toks), F32),
        jax.ShapeDtypeStruct((ff, band), F32),
        jax.ShapeDtypeStruct((ff, band), F32),
        jax.ShapeDtypeStruct((ff, band), F32),
    )
    results = pl.pallas_call(
        functools.partial(kernel, nz, ny),
        out_shape=shapes,
        in_specs=[hbm, hbm, vmem, vmem, hbm, hbm, hbm],
        out_specs=(vmem,) * 5,
        scratch_shapes=[
            pltpu.VMEM((3 * ff, width), BF),
            pltpu.VMEM((toks, quarter), BF),
            pltpu.VMEM((toks, quarter), BF),
            pltpu.VMEM((nz, ROWS, wide), BF),
            pltpu.VMEM((4, nz, ROWS, wide), BF),
            pltpu.VMEM((ny, 2, m, band), BF),
            pltpu.VMEM((ny, 2, m, band), BF),
            pltpu.VMEM((ny, m, band), BF),
            pltpu.VMEM((ny, m, band), BF),
            pltpu.VMEM((3 * ff, m), BF),
            pltpu.VMEM((3 * ff, m), BF),
            pltpu.VMEM((ny, 3 * ff, band), F32),
            pltpu.VMEM((ny, 3 * ff, band), BF),
            pltpu.VMEM((hy, 3 * ff, band), BF),
            pltpu.VMEM((hy, 3 * ff, band), BF),
            pltpu.VMEM((4, m, quarter), BF),
            pltpu.VMEM((3, m, quarter), BF),
            pltpu.VMEM((4, nz, LANES), F32),
            pltpu.VMEM((nz, ROWS, 3 * LANES), BF),
            pltpu.VMEM((nz, ROWS, 3 * LANES), BF),
            dma((7,)),
            dma((nz,)), dma((nz,)),
            dma((3, nz)), dma((3, nz)),
            dma((3,)), dma((3,)),
            dma((4,)), dma((4,)),
            dma((2, 4)), dma((2, 4)),
            dma((2, hy + 1, 4)), dma((2, hy + 1, 4)),
            dma((nz,)), dma((nz,)),
        ],
        compiler_params=pltpu.CompilerParams(
            collective_id=0, has_side_effects=True, vmem_limit_bytes=(53 * 1024 + 384) * 1024
        ),
    )(
        tokens, cotangent,
        expert_ids.reshape(1, toks), gate_probs.reshape(1, toks),
        w_gate[0].T, w_up[0].T, w_down[0],
    )
    anywhere = pl.BlockSpec(memory_space=pl.ANY)
    token_grad, prob_grad, grad_gate, grad_up, grad_down = pl.pallas_call(
        publish,
        out_shape=shapes,
        in_specs=[anywhere] * 5,
        out_specs=(anywhere,) * 5,
        scratch_shapes=[dma((5,))],
        compiler_params=pltpu.CompilerParams(vmem_limit_bytes=4 * 1024 * 1024),
    )(*results)
    return (
        token_grad, prob_grad.reshape(toks, 1),
        grad_gate.T[None], grad_up.T[None], grad_down[None],
    )


def solution(mesh):
    rows = P(("island", "ep"), None)
    in_specs = (rows, rows, rows, rows, P("ep", None, "tp"), P("ep", None, "tp"), P("ep", "tp", None))
    out_specs = (
        P(("island", "ep"), "tp"), rows,
        P("ep", "island", "tp"), P("ep", "island", "tp"), P("ep", "tp", "island"),
    )
    return jax.shard_map(shards, mesh=mesh, in_specs=in_specs, out_specs=out_specs, check_vma=False)
```

```python
import functools

import jax
import jax.numpy as jnp
from jax import lax
from jax.experimental import pallas as pl
from jax.experimental.pallas import tpu as pltpu
from jax.sharding import PartitionSpec as P

CAP = 10
ROWS = 16
SPARE = ROWS - CAP
LANES = 128
TAIL = 4 * LANES
BF = jnp.bfloat16
F32 = jnp.float32
MESH = pl.DeviceIdType.MESH
NT = ((1,), (1,))


def dot(a, b, dims=((1,), (0,)), precision=None):
    return lax.dot_general(
        a, b, (dims, ((), ())), preferred_element_type=F32, precision=precision
    )


def iota(shape, dim):
    return lax.broadcasted_iota(jnp.int32, shape, dim)


def hot(condition):
    return jnp.where(condition, 1.0, 0.0).astype(BF)


def hops(nz):
    return [d for near in range(1, nz // 2) for d in (near, nz - near)] + [nz // 2]


def kernel(
    nz, ny,
    tok, cot, ids_ref, probs_ref, wg, wu, wd,
    tg_ref, pg_ref, gg_ref, gu_ref, gd_ref,
    w, tq, cq, sb, rb, xs, ds, mx, md, gt, mgt, ch, cs, yl, yr, ip, xq, pk, rs, rr,
    ld, zs, zr, fs, fr, ms, mr, ps, pr, hs, hr, ys, yrs, vs, vr,
):
    t, z, island = lax.axis_index("tp"), lax.axis_index("ep"), lax.axis_index("island")
    y = lax.div(island, 2)
    core = island - 2 * y
    toks, quarter = tq.shape
    ff = wg.shape[0]
    m = nz * CAP
    n = nz * ROWS
    half = m // 2
    band = xs.shape[3]
    pairs = xs.shape[0]
    hz, hy = nz // 2, ny // 2
    piece_rows = 3 * ff // 4

    def tp_at(r):
        return {"tp": lax.rem(t + r, 4)}

    def ep_at(d):
        return {"ep": lax.rem(z + d, nz)}

    def y_at(d):
        return {"island": 2 * lax.rem(y + d, ny) + core}

    mate = {"island": 2 * y + 1 - core}

    def remote(src, dst, ssem, rsem, device):
        return pltpu.make_async_remote_copy(
            src_ref=src, dst_ref=dst, send_sem=ssem, recv_sem=rsem,
            device_id=device, device_id_type=MESH,
        )

    loads = [
        pltpu.make_async_copy(tok.at[:, pl.ds(pl.multiple_of(t * quarter, quarter), quarter)], tq, ld.at[0]),
        pltpu.make_async_copy(cot.at[:, pl.ds(pl.multiple_of(t * quarter, quarter), quarter)], cq, ld.at[1]),
        pltpu.make_async_copy(wg, w.at[pl.ds(0, ff)], ld.at[2]),
        pltpu.make_async_copy(wu, w.at[pl.ds(ff, ff)], ld.at[3]),
        pltpu.make_async_copy(wd, w.at[pl.ds(2 * ff, ff)], ld.at[4]),
    ]
    for copy in loads:
        copy.start()

    barrier = pltpu.get_barrier_semaphore()
    peers = [ep_at(d) for d in range(1, nz)] + [tp_at(r) for r in (1, 2, 3)]
    peers += [y_at(1), y_at(ny - 1), mate]
    for peer in peers:
        pl.semaphore_signal(barrier, inc=1, device_id=peer, device_id_type=MESH)

    ids = ids_ref[...]
    probs = probs_ref[...]
    named = hot(iota((nz, toks), 0) == ids)
    earlier = hot(iota((toks, toks), 0) < iota((toks, toks), 1))
    rank = jnp.sum(named.astype(F32) * dot(named, earlier), 0, keepdims=True)
    eye = iota((toks, toks), 0) == iota((toks, toks), 1)

    def column(row):
        return jnp.sum(jnp.where(eye, row, 0.0), 1, keepdims=True)

    probs_col = column(probs)
    ids_col = column(ids.astype(F32)).astype(jnp.int32)
    rank_col = column(rank).astype(jnp.int32)
    rank = rank.astype(jnp.int32)

    place = iota((n, toks), 0)
    block, row = lax.shift_right_logical(place, 4), place & (ROWS - 1)
    mine = block == ids
    pick_x = hot(mine & (row == rank))
    pick_d = hot(mine & (row == rank + CAP))
    piece = lax.shift_right_logical(row, 2)
    late = mine & ((row & 3) + SPARE == rank)
    pick_tail = [hot(late & (piece == c)) for c in range(4)]

    loads[0].wait()
    loads[1].wait()
    own_x = tq[...]
    own_d = (cq[...].astype(F32) * probs_col).astype(BF)
    main = dot(jnp.concatenate([pick_x, pick_d], 1), jnp.concatenate([own_x, own_d], 0))
    tail = dot(
        jnp.concatenate(pick_tail, 1),
        jnp.concatenate([own_d[:, LANES * c : LANES * (c + 1)] for c in range(4)], 0),
    )
    sb[:, :, 0:quarter] = main.astype(BF).reshape(nz, ROWS, quarter)
    sb[:, :, quarter : quarter + LANES] = tail.astype(BF).reshape(nz, ROWS, LANES)

    pl.semaphore_wait(barrier, len(peers))

    order = hops(nz)

    def z_copy(k):
        d = order[k]
        return remote(sb.at[lax.rem(z + d, nz)], rb.at[t, k + 1], zs.at[k], zr.at[k], ep_at(d))

    z_copies = [z_copy(k) for k in range(nz - 1)]
    own_block = pltpu.make_async_copy(sb.at[z], rb.at[t, 0], ld.at[5])
    own_block.start()
    for copy in reversed(z_copies):
        copy.start()

    left_q, right_q, far_q = lax.rem(t + 3, 4), lax.rem(t + 1, 4), lax.rem(t + 2, 4)

    def pass_right(p):
        return remote(rb.at[t, p], rb.at[t, p], fs.at[0, p], fr.at[0, p], tp_at(1))

    def pass_left(p):
        return remote(rb.at[t, p], rb.at[t, p], fs.at[1, p], fr.at[1, p], tp_at(3))

    def from_left(p):
        return remote(rb.at[t, p], rb.at[left_q, p], fs.at[0, p], fr.at[0, p], tp_at(1))

    def from_right(p):
        return remote(rb.at[t, p], rb.at[right_q, p], fs.at[1, p], fr.at[1, p], tp_at(3))

    direct = nz - 4 if nz > 8 else nz // 2

    def onward(p):
        if p >= direct:
            return remote(rb.at[t, p], rb.at[t, p], fs.at[2, p], fr.at[2, p], tp_at(2))
        q, to = (right_q, 3) if p % 2 else (left_q, 1)
        return remote(rb.at[q, p], rb.at[q, p], fs.at[2, p], fr.at[2, p], tp_at(to))

    def from_far(p):
        return remote(rb.at[t, p], rb.at[far_q, p], fs.at[2, p], fr.at[2, p], tp_at(1))

    def relay(p):
        from_left(p).wait_recv()
        from_right(p).wait_recv()
        onward(p).start()

    behind = 4
    for p in range(nz):
        if p == 0:
            own_block.wait()
        else:
            z_copies[p - 1].wait_recv()
        if p >= direct:
            onward(p).start()
        pass_right(p).start()
        pass_left(p).start()
        if 0 <= p - behind < direct:
            relay(p - behind)
    for p in range(max(0, nz - behind), direct):
        relay(p)

    rows = iota((half, n // 2), 0)
    source = lax.shift_right_logical(rows * 6554, 16)
    slot = rows - CAP * source
    there = iota((half, n // 2), 1)
    unpick_x = hot(there == ROWS * source + slot)
    unpick_d = hot((slot < SPARE) & (there == ROWS * source + CAP + slot))
    unpick_tail = [
        hot((slot >= SPARE) & (there == ROWS * source + 4 * c + slot - SPARE)) for c in range(4)
    ]
    unpick_main = jnp.concatenate([unpick_x, unpick_d], 0)
    unpick_tail = jnp.concatenate(unpick_tail, 0)
    per = quarter // band
    for g in range(2):
        for p in range(g * hz, g * hz + hz):
            if p >= direct:
                from_left(p).wait_recv()
                from_right(p).wait_recv()
            from_far(p).wait_recv()
        here = pl.ds(g * half, half)
        for q in range(4):
            got = rb[q, pl.ds(g * hz, hz)].reshape(n // 2, quarter + LANES)
            both = dot(unpick_main, got[:, 0:quarter])
            ends = dot(unpick_tail, got[:, quarter : quarter + LANES])
            ends = jnp.concatenate([ends[half * c : half * (c + 1)] for c in range(4)], 1)
            x_rows = both[0:half].astype(BF)
            d_rows = (both[half : 2 * half] + ends).astype(BF)
            for b in range(per):
                at = q * per + b
                xs[at // 2, at % 2, here, :] = x_rows[:, band * b : band * (b + 1)]
                ds[at // 2, at % 2, here, :] = d_rows[:, band * b : band * (b + 1)]

    mate_x = remote(xs.at[:, 1 - core], mx, ms.at[0], mr.at[0], mate)
    mate_d = remote(ds.at[:, 1 - core], md, ms.at[1], mr.at[1], mate)
    mate_g = remote(gt, mgt, ms.at[2], mr.at[2], mate)
    mate_x.start()
    mate_d.start()

    for copy in loads[2:]:
        copy.wait()
    x_all = jnp.concatenate([xs[o, c] for o in range(pairs) for c in range(2)], 1)
    d_all = jnp.concatenate([ds[o, c] for o in range(pairs) for c in range(2)], 1)
    gate_up = dot(w[0 : 2 * ff, :], x_all, NT)
    back = dot(w[2 * ff : 3 * ff, :], d_all, NT)
    gate, up = gate_up[0:ff], gate_up[ff : 2 * ff]
    sigma = jax.nn.sigmoid(gate)
    active = gate * sigma
    hidden = (active * up).astype(BF)
    gt[0:ff, :] = (back * up * sigma * (1.0 + gate * (1.0 - sigma))).astype(BF)
    gt[ff : 2 * ff, :] = (back * active).astype(BF)
    gt[2 * ff : 3 * ff, :] = hidden
    mate_g.start()

    eye_m = hot(iota((m, m), 0) == iota((m, m), 1))
    d_rows = dot(eye_m, gt[0 : 2 * ff, :], NT).astype(BF)

    def input_part(r):
        q = lax.rem(t + r, 4)
        cols = pl.ds(pl.multiple_of(q * quarter, quarter), quarter)
        ip[r] = dot(d_rows, w[0 : 2 * ff, cols]).astype(BF)

    def tp_copy(g, r):
        here = pl.ds(g * half, half)
        return remote(ip.at[r, here], xq.at[r - 1, here], hs.at[g, r], hr.at[g, r], tp_at(r))

    tp_copies = [[tp_copy(g, r) for r in (1, 2, 3)] for g in range(2)]

    def weight_part(*js):
        def cat(blocks):
            return blocks[0] if len(blocks) == 1 else jnp.concatenate(blocks, 1)

        os = [lax.rem(y + j, ny) for j in js]
        top = dot(gt[0 : 2 * ff, :], cat([xs[o, core] for o in os]))
        top = top + dot(mgt[0 : 2 * ff, :], cat([mx[o] for o in os]))
        low = dot(gt[2 * ff : 3 * ff, :], cat([ds[o, core] for o in os]))
        low = low + dot(mgt[2 * ff : 3 * ff, :], cat([md[o] for o in os]))
        for i, j in enumerate(js):
            ch[j, 0 : 2 * ff, :] = top[:, band * i : band * (i + 1)]
            ch[j, 2 * ff : 3 * ff, :] = low[:, band * i : band * (i + 1)]

    def y_copy(side, dist, part):
        j = dist if side == 0 else ny - dist
        where = pl.ds(part * piece_rows, piece_rows)
        into = (yl, yr)[side]
        return remote(
            cs.at[j, where], into.at[dist - 1, where],
            ys.at[side, dist, part], yrs.at[side, dist, part], y_at(1 if side == 0 else ny - 1),
        )

    far_parts, near_parts = ((0, 1), (2, 3)), ((2, 3), (0, 1))

    def y_step(side, dist, part):
        j = dist if side == 0 else ny - dist
        where = pl.ds(part * piece_rows, piece_rows)
        if dist == hy or (dist == hy - 1 and part in near_parts[side]):
            cs[j, where, :] = ch[j, where, :].astype(BF)
        else:
            y_copy(side, dist + 1, part).wait_recv()
            came = (yl, yr)[side][dist, where, :].astype(F32)
            cs[j, where, :] = (ch[j, where, :] + came).astype(BF)
        y_copy(side, dist, part).start()

    def y_steps(dist, parts):
        for i in range(2):
            for side in (0, 1):
                y_step(side, dist, parts[side][i])

    for r in (2, 1, 3):
        input_part(r)
        tp_copies[1][r - 1].start()
    for r in (2, 1, 3):
        tp_copies[0][r - 1].start()

    input_part(0)
    prob_row = jnp.sum(hidden.astype(F32) * back, 0, keepdims=True)
    in_source = iota((nz, m), 0) == lax.shift_right_logical(iota((nz, m), 1) * 6554, 16)
    at_row = iota((m, LANES), 0)
    at_slot = iota((m, LANES), 1) == at_row - CAP * lax.shift_right_logical(at_row * 6554, 16)
    pk[0] = dot(
        jnp.where(in_source, prob_row, 0.0), jnp.where(at_slot, 1.0, 0.0),
        precision=lax.Precision.HIGHEST,
    )
    prob_sends = [remote(pk.at[0], pk.at[r], ps.at[r], pr.at[r], tp_at(r)) for r in (1, 2, 3)]
    for copy in prob_sends:
        copy.start()

    mate_x.wait_recv()
    mate_d.wait_recv()
    mate_g.wait_recv()
    weight_part(hy)
    y_steps(hy, far_parts)
    weight_part(hy - 1, ny - hy + 1)
    y_steps(hy - 1, near_parts)
    if hy > 2:
        weight_part(hy - 2, ny - hy + 2)
    y_steps(hy - 1, far_parts)

    for copy in prob_sends:
        copy.wait_recv()
    prob = (pk[0] + pk[1]) + (pk[2] + pk[3])
    prob_high = prob.astype(BF)
    prob_low = (prob - prob_high.astype(F32)).astype(BF)
    to = iota((n // 2, half), 0)
    block, row = lax.shift_right_logical(to, 4), to & (ROWS - 1)
    first = CAP * block
    frm = iota((n // 2, half), 1)
    pack = hot((row < CAP) & (frm == first + row))
    pack_0 = hot((row >= CAP) & (frm == first + row - CAP))
    pack_1 = hot((row >= CAP) & (row < ROWS - 2) & (frm == first + row - CAP + SPARE))
    to = iota((n // 2, nz), 0)
    block, row = lax.shift_right_logical(to, 4), to & (ROWS - 1)

    def back_copy(k):
        d = nz - order[k]
        return remote(rs.at[k + 1], rr.at[z], vs.at[k], vr.at[k], ep_at(d))

    def back_recv(k):
        return remote(rs.at[0], rr.at[lax.rem(z + order[k], nz)], vs.at[k], vr.at[k], ep_at(1))

    def send_back(g):
        for copy in tp_copies[g]:
            copy.wait_recv()
        here = pl.ds(g * half, half)
        summed = ip[0, here, :].astype(F32) + xq[0, here, :].astype(F32)
        summed = summed + (xq[1, here, :].astype(F32) + xq[2, here, :].astype(F32))
        summed = summed.astype(BF)
        ends = summed[:, 3 * LANES : 4 * LANES]
        same = block + g * hz == iota((n // 2, nz), 1)
        extra = dot(hot(same & (row == CAP)), prob_high) + dot(hot(same & (row == CAP + 1)), prob_low)
        packed = dot(pack, summed[:, 0 : 3 * LANES])
        packed = packed + jnp.concatenate([dot(pack_0, ends), dot(pack_1, ends), extra], 1)
        rs[pl.ds(g * hz, hz)] = packed.astype(BF).reshape(hz, ROWS, 3 * LANES)
        for k in reversed(range(max(g * hz - 1, 0), g * hz + hz - 1)):
            back_copy(k).start()

    send_back(1)
    for dist in range(hy - 2, 0, -1):
        y_steps(dist, near_parts)
        if dist > 1:
            weight_part(dist - 1, ny - dist + 1)
            y_steps(dist, far_parts)
    send_back(0)
    own_back = pltpu.make_async_copy(rs.at[0], rr.at[z], ld.at[6])
    own_back.start()
    if hy > 2:
        y_steps(1, far_parts)
    weight_part(0)
    for parts_at in (near_parts, far_parts):
        for i in range(2):
            for side in (0, 1):
                y_copy(side, 1, parts_at[side][i]).wait_recv()
    total = ch[0] + (yl[0].astype(F32) + yr[0].astype(F32))
    gg_ref[...] = total[0:ff]
    gu_ref[...] = total[ff : 2 * ff]
    gd_ref[...] = total[2 * ff : 3 * ff]

    at = iota((toks, n), 1)
    block, row = lax.shift_right_logical(at, 4), at & (ROWS - 1)
    mine = block == ids_col
    take = hot(mine & (row == rank_col))
    take_0 = hot(mine & (row == rank_col + CAP) & (rank_col < SPARE))
    take_1 = hot(mine & (row == rank_col + CAP - SPARE) & (rank_col >= SPARE))
    take_high, take_low = hot(mine & (row == CAP)), hot(mine & (row == CAP + 1))

    for k in range(nz - 1):
        back_recv(k).wait_recv()
    own_back.wait()
    got = rr[...].reshape(n, 3 * LANES)
    tg_ref[:, 0 : 3 * LANES] = dot(take, got).astype(BF)
    tg_ref[:, 3 * LANES : 4 * LANES] = (
        dot(take_0, got[:, 0:LANES]) + dot(take_1, got[:, LANES : 2 * LANES])
    ).astype(BF)
    ends = got[:, 2 * LANES : 3 * LANES]
    chosen = iota((toks, LANES), 1) == rank_col
    value = jnp.where(chosen, dot(take_high, ends) + dot(take_low, ends), 0.0)
    value = jnp.sum(value, 1, keepdims=True) / probs_col
    pg_ref[...] = jnp.sum(jnp.where(eye, value, 0.0), 0, keepdims=True)

    for k in range(nz - 1):
        z_copies[k].wait_send()
        back_copy(k).wait_send()
    for p in range(nz):
        pass_right(p).wait_send()
        pass_left(p).wait_send()
        onward(p).wait_send()
    for copy in [mate_x, mate_d, mate_g] + prob_sends:
        copy.wait_send()
    for copy in tp_copies[0] + tp_copies[1]:
        copy.wait_send()
    for side in (0, 1):
        for part in far_parts[side]:
            y_copy(side, hy, part).wait_send()
        for dist in range(hy - 1, 0, -1):
            for part in range(4):
                y_copy(side, dist, part).wait_send()


def publish(*refs):
    copies = [pltpu.make_async_copy(refs[i], refs[i + 5], refs[10].at[i]) for i in range(5)]
    for copy in copies:
        copy.start()
    for copy in copies:
        copy.wait()


def shards(tokens, cotangent, expert_ids, gate_probs, w_gate, w_up, w_down):
    toks, width = tokens.shape
    ff = w_down.shape[1]
    nz, ny = lax.axis_size("ep"), lax.axis_size("island") // 2
    quarter, band = width // 4, width // (2 * ny)
    m = nz * CAP
    wide = quarter + LANES
    hy, hz = ny // 2, nz // 2
    hbm = pl.BlockSpec(memory_space=pltpu.HBM)
    vmem = pl.BlockSpec(memory_space=pltpu.VMEM)
    dma = pltpu.SemaphoreType.DMA
    shapes = (
        jax.ShapeDtypeStruct((toks, quarter), BF),
        jax.ShapeDtypeStruct((1, toks), F32),
        jax.ShapeDtypeStruct((ff, band), F32),
        jax.ShapeDtypeStruct((ff, band), F32),
        jax.ShapeDtypeStruct((ff, band), F32),
    )
    results = pl.pallas_call(
        functools.partial(kernel, nz, ny),
        out_shape=shapes,
        in_specs=[hbm, hbm, vmem, vmem, hbm, hbm, hbm],
        out_specs=(vmem,) * 5,
        scratch_shapes=[
            pltpu.VMEM((3 * ff, width), BF),
            pltpu.VMEM((toks, quarter), BF),
            pltpu.VMEM((toks, quarter), BF),
            pltpu.VMEM((nz, ROWS, wide), BF),
            pltpu.VMEM((4, nz, ROWS, wide), BF),
            pltpu.VMEM((ny, 2, m, band), BF),
            pltpu.VMEM((ny, 2, m, band), BF),
            pltpu.VMEM((ny, m, band), BF),
            pltpu.VMEM((ny, m, band), BF),
            pltpu.VMEM((3 * ff, m), BF),
            pltpu.VMEM((3 * ff, m), BF),
            pltpu.VMEM((ny, 3 * ff, band), F32),
            pltpu.VMEM((ny, 3 * ff, band), BF),
            pltpu.VMEM((hy, 3 * ff, band), BF),
            pltpu.VMEM((hy, 3 * ff, band), BF),
            pltpu.VMEM((4, m, quarter), BF),
            pltpu.VMEM((3, m, quarter), BF),
            pltpu.VMEM((4, nz, LANES), F32),
            pltpu.VMEM((nz, ROWS, 3 * LANES), BF),
            pltpu.VMEM((nz, ROWS, 3 * LANES), BF),
            dma((7,)),
            dma((nz,)), dma((nz,)),
            dma((3, nz)), dma((3, nz)),
            dma((3,)), dma((3,)),
            dma((4,)), dma((4,)),
            dma((2, 4)), dma((2, 4)),
            dma((2, hy + 1, 4)), dma((2, hy + 1, 4)),
            dma((nz,)), dma((nz,)),
        ],
        compiler_params=pltpu.CompilerParams(
            collective_id=0, has_side_effects=True, vmem_limit_bytes=(53 * 1024 + 384) * 1024
        ),
    )(
        tokens, cotangent,
        expert_ids.reshape(1, toks), gate_probs.reshape(1, toks),
        w_gate[0].T, w_up[0].T, w_down[0],
    )
    anywhere = pl.BlockSpec(memory_space=pl.ANY)
    token_grad, prob_grad, grad_gate, grad_up, grad_down = pl.pallas_call(
        publish,
        out_shape=shapes,
        in_specs=[anywhere] * 5,
        out_specs=(anywhere,) * 5,
        scratch_shapes=[dma((5,))],
        compiler_params=pltpu.CompilerParams(vmem_limit_bytes=4 * 1024 * 1024),
    )(*results)
    return (
        token_grad, prob_grad.reshape(toks, 1),
        grad_gate.T[None], grad_up.T[None], grad_down[None],
    )


def solution(mesh):
    rows = P(("island", "ep"), None)
    in_specs = (rows, rows, rows, rows, P("ep", None, "tp"), P("ep", None, "tp"), P("ep", "tp", None))
    out_specs = (
        P(("island", "ep"), "tp"), rows,
        P("ep", "island", "tp"), P("ep", "island", "tp"), P("ep", "tp", "island"),
    )
    return jax.shard_map(shards, mesh=mesh, in_specs=in_specs, out_specs=out_specs, check_vma=False)
```

```python
import functools

import jax
import jax.numpy as jnp
from jax import lax
from jax.experimental import pallas as pl
from jax.experimental.pallas import tpu as pltpu
from jax.sharding import PartitionSpec as P

CAP = 10
ROWS = 16
SPARE = ROWS - CAP
LANES = 128
TAIL = 4 * LANES
BF = jnp.bfloat16
F32 = jnp.float32
MESH = pl.DeviceIdType.MESH
NT = ((1,), (1,))


def dot(a, b, dims=((1,), (0,)), precision=None):
    return lax.dot_general(
        a, b, (dims, ((), ())), preferred_element_type=F32, precision=precision
    )


def iota(shape, dim):
    return lax.broadcasted_iota(jnp.int32, shape, dim)


def hot(condition):
    return jnp.where(condition, 1.0, 0.0).astype(BF)


def hops(nz):
    near = [1, 2] if nz > 8 else []
    pairs = []
    for d in range(nz // 2 - 1, len(near), -1):
        pairs += [d] + near[len(pairs) // 2 : len(pairs) // 2 + 1]
    return [nz // 2] + [d for pair in pairs for d in (pair, nz - pair)]


def kernel(
    nz, ny,
    tok, cot, ids_ref, probs_ref, wg, wu, wd,
    tg_ref, pg_ref, gg_ref, gu_ref, gd_ref,
    w, tq, cq, sb, rb, xs, ds, mx, md, gt, mgt, ch, cs, yl, yr, ip, xq, pk, rs, rr,
    ld, zs, zr, fs, fr, ms, mr, ps, pr, hs, hr, ys, yrs, vs, vr,
):
    t, z, island = lax.axis_index("tp"), lax.axis_index("ep"), lax.axis_index("island")
    y = lax.div(island, 2)
    core = island - 2 * y
    toks, quarter = tq.shape
    ff = wg.shape[0]
    m = nz * CAP
    n = nz * ROWS
    half = m // 2
    band = xs.shape[3]
    pairs = xs.shape[0]
    hz, hy = nz // 2, ny // 2
    piece_rows = 3 * ff // 4

    def tp_at(r):
        return {"tp": lax.rem(t + r, 4)}

    def ep_at(d):
        return {"ep": lax.rem(z + d, nz)}

    def y_at(d):
        return {"island": 2 * lax.rem(y + d, ny) + core}

    mate = {"island": 2 * y + 1 - core}

    def remote(src, dst, ssem, rsem, device):
        return pltpu.make_async_remote_copy(
            src_ref=src, dst_ref=dst, send_sem=ssem, recv_sem=rsem,
            device_id=device, device_id_type=MESH,
        )

    loads = [
        pltpu.make_async_copy(tok.at[:, pl.ds(pl.multiple_of(t * quarter, quarter), quarter)], tq, ld.at[0]),
        pltpu.make_async_copy(cot.at[:, pl.ds(pl.multiple_of(t * quarter, quarter), quarter)], cq, ld.at[1]),
        pltpu.make_async_copy(wg, w.at[pl.ds(0, ff)], ld.at[2]),
        pltpu.make_async_copy(wu, w.at[pl.ds(ff, ff)], ld.at[3]),
        pltpu.make_async_copy(wd, w.at[pl.ds(2 * ff, ff)], ld.at[4]),
    ]
    for copy in loads:
        copy.start()

    barrier = pltpu.get_barrier_semaphore()
    peers = [ep_at(d) for d in range(1, nz)] + [tp_at(r) for r in (1, 2, 3)]
    peers += [y_at(1), y_at(ny - 1), mate]
    for peer in peers:
        pl.semaphore_signal(barrier, inc=1, device_id=peer, device_id_type=MESH)

    ids = ids_ref[...]
    probs = probs_ref[...]
    named = hot(iota((nz, toks), 0) == ids)
    earlier = hot(iota((toks, toks), 0) < iota((toks, toks), 1))
    rank = jnp.sum(named.astype(F32) * dot(named, earlier), 0, keepdims=True)
    eye = iota((toks, toks), 0) == iota((toks, toks), 1)

    def column(row):
        return jnp.sum(jnp.where(eye, row, 0.0), 1, keepdims=True)

    probs_col = column(probs)
    ids_col = column(ids.astype(F32)).astype(jnp.int32)
    rank_col = column(rank).astype(jnp.int32)
    rank = rank.astype(jnp.int32)

    place = iota((n, toks), 0)
    block, row = lax.shift_right_logical(place, 4), place & (ROWS - 1)
    mine = block == ids
    pick_x = hot(mine & (row == rank))
    pick_d = hot(mine & (row == rank + CAP))
    piece = lax.shift_right_logical(row, 2)
    late = mine & ((row & 3) + SPARE == rank)
    pick_tail = [hot(late & (piece == c)) for c in range(4)]

    loads[0].wait()
    loads[1].wait()
    own_x = tq[...]
    own_d = (cq[...].astype(F32) * probs_col).astype(BF)
    main = dot(jnp.concatenate([pick_x, pick_d], 1), jnp.concatenate([own_x, own_d], 0))
    tail = dot(
        jnp.concatenate(pick_tail, 1),
        jnp.concatenate([own_d[:, LANES * c : LANES * (c + 1)] for c in range(4)], 0),
    )
    sb[:, :, 0:quarter] = main.astype(BF).reshape(nz, ROWS, quarter)
    sb[:, :, quarter : quarter + LANES] = tail.astype(BF).reshape(nz, ROWS, LANES)

    pl.semaphore_wait(barrier, len(peers))

    order = hops(nz)

    def z_copy(k):
        d = order[k]
        return remote(sb.at[lax.rem(z + d, nz)], rb.at[t, k + 1], zs.at[k], zr.at[k], ep_at(d))

    z_copies = [z_copy(k) for k in range(nz - 1)]
    own_block = pltpu.make_async_copy(sb.at[z], rb.at[t, 0], ld.at[5])
    own_block.start()
    for copy in z_copies:
        copy.start()

    left_q, right_q, far_q = lax.rem(t + 3, 4), lax.rem(t + 1, 4), lax.rem(t + 2, 4)

    def pass_right(p):
        return remote(rb.at[t, p], rb.at[t, p], fs.at[0, p], fr.at[0, p], tp_at(1))

    def pass_left(p):
        return remote(rb.at[t, p], rb.at[t, p], fs.at[1, p], fr.at[1, p], tp_at(3))

    def from_left(p):
        return remote(rb.at[t, p], rb.at[left_q, p], fs.at[0, p], fr.at[0, p], tp_at(1))

    def from_right(p):
        return remote(rb.at[t, p], rb.at[right_q, p], fs.at[1, p], fr.at[1, p], tp_at(3))

    direct = nz - 4 if nz > 8 else nz // 2

    def onward(p):
        if p >= direct:
            return remote(rb.at[t, p], rb.at[t, p], fs.at[2, p], fr.at[2, p], tp_at(2))
        q, to = (right_q, 3) if p % 2 else (left_q, 1)
        return remote(rb.at[q, p], rb.at[q, p], fs.at[2, p], fr.at[2, p], tp_at(to))

    def from_far(p):
        return remote(rb.at[t, p], rb.at[far_q, p], fs.at[2, p], fr.at[2, p], tp_at(1))

    def relay(p):
        from_left(p).wait_recv()
        from_right(p).wait_recv()
        onward(p).start()

    behind = 4
    for p in range(nz):
        if p == 0:
            own_block.wait()
        else:
            z_copies[p - 1].wait_recv()
        if p >= direct:
            onward(p).start()
        pass_right(p).start()
        pass_left(p).start()
        if 0 <= p - behind < direct:
            relay(p - behind)
    for p in range(max(0, nz - behind), direct):
        relay(p)

    rows = iota((half, n // 2), 0)
    source = lax.shift_right_logical(rows * 6554, 16)
    slot = rows - CAP * source
    there = iota((half, n // 2), 1)
    unpick_x = hot(there == ROWS * source + slot)
    unpick_d = hot((slot < SPARE) & (there == ROWS * source + CAP + slot))
    unpick_tail = [
        hot((slot >= SPARE) & (there == ROWS * source + 4 * c + slot - SPARE)) for c in range(4)
    ]
    unpick_main = jnp.concatenate([unpick_x, unpick_d], 0)
    unpick_tail = jnp.concatenate(unpick_tail, 0)
    per = quarter // band
    for g in range(2):
        for p in range(g * hz, g * hz + hz):
            if p >= direct:
                from_left(p).wait_recv()
                from_right(p).wait_recv()
            from_far(p).wait_recv()
        here = pl.ds(g * half, half)
        for q in range(4):
            got = rb[q, pl.ds(g * hz, hz)].reshape(n // 2, quarter + LANES)
            both = dot(unpick_main, got[:, 0:quarter])
            ends = dot(unpick_tail, got[:, quarter : quarter + LANES])
            ends = jnp.concatenate([ends[half * c : half * (c + 1)] for c in range(4)], 1)
            x_rows = both[0:half].astype(BF)
            d_rows = (both[half : 2 * half] + ends).astype(BF)
            for b in range(per):
                at = q * per + b
                xs[at // 2, at % 2, here, :] = x_rows[:, band * b : band * (b + 1)]
                ds[at // 2, at % 2, here, :] = d_rows[:, band * b : band * (b + 1)]

    mate_x = remote(xs.at[:, 1 - core], mx, ms.at[0], mr.at[0], mate)
    mate_d = remote(ds.at[:, 1 - core], md, ms.at[1], mr.at[1], mate)
    mate_g = remote(gt, mgt, ms.at[2], mr.at[2], mate)
    mate_x.start()
    mate_d.start()

    for copy in loads[2:]:
        copy.wait()
    x_all = jnp.concatenate([xs[o, c] for o in range(pairs) for c in range(2)], 1)
    d_all = jnp.concatenate([ds[o, c] for o in range(pairs) for c in range(2)], 1)
    gate_up = dot(w[0 : 2 * ff, :], x_all, NT)
    back = dot(w[2 * ff : 3 * ff, :], d_all, NT)
    gate, up = gate_up[0:ff], gate_up[ff : 2 * ff]
    sigma = jax.nn.sigmoid(gate)
    active = gate * sigma
    hidden = (active * up).astype(BF)
    gt[0:ff, :] = (back * up * sigma * (1.0 + gate * (1.0 - sigma))).astype(BF)
    gt[ff : 2 * ff, :] = (back * active).astype(BF)
    gt[2 * ff : 3 * ff, :] = hidden
    mate_g.start()

    eye_m = hot(iota((m, m), 0) == iota((m, m), 1))
    d_rows = dot(eye_m, gt[0 : 2 * ff, :], NT).astype(BF)

    def input_part(r):
        q = lax.rem(t + r, 4)
        cols = pl.ds(pl.multiple_of(q * quarter, quarter), quarter)
        ip[r] = dot(d_rows, w[0 : 2 * ff, cols]).astype(BF)

    def tp_copy(g, r):
        here = pl.ds(g * half, half)
        return remote(ip.at[r, here], xq.at[r - 1, here], hs.at[g, r], hr.at[g, r], tp_at(r))

    tp_copies = [[tp_copy(g, r) for r in (1, 2, 3)] for g in range(2)]

    def weight_part(*js):
        def cat(blocks):
            return blocks[0] if len(blocks) == 1 else jnp.concatenate(blocks, 1)

        os = [lax.rem(y + j, ny) for j in js]
        top = dot(gt[0 : 2 * ff, :], cat([xs[o, core] for o in os]))
        top = top + dot(mgt[0 : 2 * ff, :], cat([mx[o] for o in os]))
        low = dot(gt[2 * ff : 3 * ff, :], cat([ds[o, core] for o in os]))
        low = low + dot(mgt[2 * ff : 3 * ff, :], cat([md[o] for o in os]))
        for i, j in enumerate(js):
            ch[j, 0 : 2 * ff, :] = top[:, band * i : band * (i + 1)]
            ch[j, 2 * ff : 3 * ff, :] = low[:, band * i : band * (i + 1)]

    def y_copy(side, dist, part):
        j = dist if side == 0 else ny - dist
        where = pl.ds(part * piece_rows, piece_rows)
        into = (yl, yr)[side]
        return remote(
            cs.at[j, where], into.at[dist - 1, where],
            ys.at[side, dist, part], yrs.at[side, dist, part], y_at(1 if side == 0 else ny - 1),
        )

    far_parts, near_parts = ((0, 1), (2, 3)), ((2, 3), (0, 1))

    def y_step(side, dist, part):
        j = dist if side == 0 else ny - dist
        where = pl.ds(part * piece_rows, piece_rows)
        if dist == hy or (dist == hy - 1 and part in near_parts[side]):
            cs[j, where, :] = ch[j, where, :].astype(BF)
        else:
            y_copy(side, dist + 1, part).wait_recv()
            came = (yl, yr)[side][dist, where, :].astype(F32)
            cs[j, where, :] = (ch[j, where, :] + came).astype(BF)
        y_copy(side, dist, part).start()

    def y_steps(dist, parts):
        for i in range(2):
            for side in (0, 1):
                y_step(side, dist, parts[side][i])

    for r in (2, 1, 3):
        input_part(r)
        tp_copies[0][r - 1].start()
    for r in (2, 1, 3):
        tp_copies[1][r - 1].start()

    mate_x.wait_recv()
    mate_d.wait_recv()
    mate_g.wait_recv()
    weight_part(hy)
    y_steps(hy, far_parts)
    weight_part(hy - 1, ny - hy + 1)
    y_steps(hy - 1, near_parts)

    prob_row = jnp.sum(hidden.astype(F32) * back, 0, keepdims=True)
    in_source = iota((nz, m), 0) == lax.shift_right_logical(iota((nz, m), 1) * 6554, 16)
    at_row = iota((m, LANES), 0)
    at_slot = iota((m, LANES), 1) == at_row - CAP * lax.shift_right_logical(at_row * 6554, 16)
    pk[0] = dot(
        jnp.where(in_source, prob_row, 0.0), jnp.where(at_slot, 1.0, 0.0),
        precision=lax.Precision.HIGHEST,
    )
    prob_sends = [remote(pk.at[0], pk.at[r], ps.at[r], pr.at[r], tp_at(r)) for r in (1, 2, 3)]
    for copy in prob_sends:
        copy.start()
    input_part(0)
    y_steps(hy - 1, far_parts)
    if hy > 2:
        weight_part(hy - 2, ny - hy + 2)

    for copy in prob_sends:
        copy.wait_recv()
    prob = (pk[0] + pk[1]) + (pk[2] + pk[3])
    prob_high = prob.astype(BF)
    prob_low = (prob - prob_high.astype(F32)).astype(BF)
    to = iota((n // 2, half), 0)
    block, row = lax.shift_right_logical(to, 4), to & (ROWS - 1)
    first = CAP * block
    frm = iota((n // 2, half), 1)
    pack = hot((row < CAP) & (frm == first + row))
    pack_0 = hot((row >= CAP) & (frm == first + row - CAP))
    pack_1 = hot((row >= CAP) & (row < ROWS - 2) & (frm == first + row - CAP + SPARE))
    to = iota((n // 2, nz), 0)
    block, row = lax.shift_right_logical(to, 4), to & (ROWS - 1)

    def back_copy(k):
        d = nz - order[k]
        return remote(rs.at[k + 1], rr.at[z], vs.at[k], vr.at[k], ep_at(d))

    def back_recv(k):
        return remote(rs.at[0], rr.at[lax.rem(z + order[k], nz)], vs.at[k], vr.at[k], ep_at(1))

    def send_back(g):
        for copy in tp_copies[g]:
            copy.wait_recv()
        here = pl.ds(g * half, half)
        summed = ip[0, here, :].astype(F32) + xq[0, here, :].astype(F32)
        summed = summed + (xq[1, here, :].astype(F32) + xq[2, here, :].astype(F32))
        summed = summed.astype(BF)
        ends = summed[:, 3 * LANES : 4 * LANES]
        same = block + g * hz == iota((n // 2, nz), 1)
        extra = dot(hot(same & (row == CAP)), prob_high) + dot(hot(same & (row == CAP + 1)), prob_low)
        packed = dot(pack, summed[:, 0 : 3 * LANES])
        packed = packed + jnp.concatenate([dot(pack_0, ends), dot(pack_1, ends), extra], 1)
        rs[pl.ds(g * hz, hz)] = packed.astype(BF).reshape(hz, ROWS, 3 * LANES)
        for k in range(max(g * hz - 1, 0), g * hz + hz - 1):
            back_copy(k).start()

    send_back(0)
    if hy > 2:
        y_steps(hy - 2, near_parts)
    send_back(1)
    own_back = pltpu.make_async_copy(rs.at[0], rr.at[z], ld.at[6])
    own_back.start()
    for dist in range(hy - 2, 0, -1):
        if dist < hy - 2:
            y_steps(dist, near_parts)
        else:
            for at in range(dist - 1, 0, -1):
                weight_part(at, ny - at)
        y_steps(dist, far_parts)
    weight_part(0)

    for copy in z_copies + [mate_x, mate_d, mate_g] + prob_sends + tp_copies[0] + tp_copies[1]:
        copy.wait_send()
    for p in range(nz):
        pass_right(p).wait_send()
        pass_left(p).wait_send()
        onward(p).wait_send()
    for side in (0, 1):
        for dist in range(hy, 1, -1):
            for part in range(4):
                if dist < hy or part in far_parts[side]:
                    y_copy(side, dist, part).wait_send()
    for parts_at in (near_parts, far_parts):
        for i in range(2):
            for side in (0, 1):
                y_copy(side, 1, parts_at[side][i]).wait_recv()
    total = ch[0] + (yl[0].astype(F32) + yr[0].astype(F32))
    gg_ref[...] = total[0:ff]
    gu_ref[...] = total[ff : 2 * ff]
    gd_ref[...] = total[2 * ff : 3 * ff]

    at = iota((toks, n), 1)
    block, row = lax.shift_right_logical(at, 4), at & (ROWS - 1)
    mine = block == ids_col
    take = hot(mine & (row == rank_col))
    take_0 = hot(mine & (row == rank_col + CAP) & (rank_col < SPARE))
    take_1 = hot(mine & (row == rank_col + CAP - SPARE) & (rank_col >= SPARE))
    take_high, take_low = hot(mine & (row == CAP)), hot(mine & (row == CAP + 1))

    for k in range(nz - 1):
        back_recv(k).wait_recv()
    own_back.wait()
    got = rr[...].reshape(n, 3 * LANES)
    tg_ref[:, 0 : 3 * LANES] = dot(take, got).astype(BF)
    tg_ref[:, 3 * LANES : 4 * LANES] = (
        dot(take_0, got[:, 0:LANES]) + dot(take_1, got[:, LANES : 2 * LANES])
    ).astype(BF)
    ends = got[:, 2 * LANES : 3 * LANES]
    chosen = iota((toks, LANES), 1) == rank_col
    value = jnp.where(chosen, dot(take_high, ends) + dot(take_low, ends), 0.0)
    value = jnp.sum(value, 1, keepdims=True) / probs_col
    pg_ref[...] = jnp.sum(jnp.where(eye, value, 0.0), 0, keepdims=True)

    for k in range(nz - 1):
        back_copy(k).wait_send()
    for side in (0, 1):
        for part in range(4):
            if hy > 1 or part in far_parts[side]:
                y_copy(side, 1, part).wait_send()


def publish(*refs):
    copies = [pltpu.make_async_copy(refs[i], refs[i + 5], refs[10].at[i]) for i in range(5)]
    for copy in copies:
        copy.start()
    for copy in copies:
        copy.wait()


def shards(tokens, cotangent, expert_ids, gate_probs, w_gate, w_up, w_down):
    toks, width = tokens.shape
    ff = w_down.shape[1]
    nz, ny = lax.axis_size("ep"), lax.axis_size("island") // 2
    quarter, band = width // 4, width // (2 * ny)
    m = nz * CAP
    wide = quarter + LANES
    hy, hz = ny // 2, nz // 2
    hbm = pl.BlockSpec(memory_space=pltpu.HBM)
    vmem = pl.BlockSpec(memory_space=pltpu.VMEM)
    dma = pltpu.SemaphoreType.DMA
    shapes = (
        jax.ShapeDtypeStruct((toks, quarter), BF),
        jax.ShapeDtypeStruct((1, toks), F32),
        jax.ShapeDtypeStruct((ff, band), F32),
        jax.ShapeDtypeStruct((ff, band), F32),
        jax.ShapeDtypeStruct((ff, band), F32),
    )
    results = pl.pallas_call(
        functools.partial(kernel, nz, ny),
        out_shape=shapes,
        in_specs=[hbm, hbm, vmem, vmem, hbm, hbm, hbm],
        out_specs=(vmem,) * 5,
        scratch_shapes=[
            pltpu.VMEM((3 * ff, width), BF),
            pltpu.VMEM((toks, quarter), BF),
            pltpu.VMEM((toks, quarter), BF),
            pltpu.VMEM((nz, ROWS, wide), BF),
            pltpu.VMEM((4, nz, ROWS, wide), BF),
            pltpu.VMEM((ny, 2, m, band), BF),
            pltpu.VMEM((ny, 2, m, band), BF),
            pltpu.VMEM((ny, m, band), BF),
            pltpu.VMEM((ny, m, band), BF),
            pltpu.VMEM((3 * ff, m), BF),
            pltpu.VMEM((3 * ff, m), BF),
            pltpu.VMEM((ny, 3 * ff, band), F32),
            pltpu.VMEM((ny, 3 * ff, band), BF),
            pltpu.VMEM((hy, 3 * ff, band), BF),
            pltpu.VMEM((hy, 3 * ff, band), BF),
            pltpu.VMEM((4, m, quarter), BF),
            pltpu.VMEM((3, m, quarter), BF),
            pltpu.VMEM((4, nz, LANES), F32),
            pltpu.VMEM((nz, ROWS, 3 * LANES), BF),
            pltpu.VMEM((nz, ROWS, 3 * LANES), BF),
            dma((7,)),
            dma((nz,)), dma((nz,)),
            dma((3, nz)), dma((3, nz)),
            dma((3,)), dma((3,)),
            dma((4,)), dma((4,)),
            dma((2, 4)), dma((2, 4)),
            dma((2, hy + 1, 4)), dma((2, hy + 1, 4)),
            dma((nz,)), dma((nz,)),
        ],
        compiler_params=pltpu.CompilerParams(
            collective_id=0, has_side_effects=True, vmem_limit_bytes=(53 * 1024 + 384) * 1024
        ),
    )(
        tokens, cotangent,
        expert_ids.reshape(1, toks), gate_probs.reshape(1, toks),
        w_gate[0].T, w_up[0].T, w_down[0],
    )
    anywhere = pl.BlockSpec(memory_space=pl.ANY)
    token_grad, prob_grad, grad_gate, grad_up, grad_down = pl.pallas_call(
        publish,
        out_shape=shapes,
        in_specs=[anywhere] * 5,
        out_specs=(anywhere,) * 5,
        scratch_shapes=[dma((5,))],
        compiler_params=pltpu.CompilerParams(vmem_limit_bytes=4 * 1024 * 1024),
    )(*results)
    return (
        token_grad, prob_grad.reshape(toks, 1),
        grad_gate.T[None], grad_up.T[None], grad_down[None],
    )


def solution(mesh):
    rows = P(("island", "ep"), None)
    in_specs = (rows, rows, rows, rows, P("ep", None, "tp"), P("ep", None, "tp"), P("ep", "tp", None))
    out_specs = (
        P(("island", "ep"), "tp"), rows,
        P("ep", "island", "tp"), P("ep", "island", "tp"), P("ep", "tp", "island"),
    )
    return jax.shard_map(shards, mesh=mesh, in_specs=in_specs, out_specs=out_specs, check_vma=False)
```

```python
import functools

import jax
import jax.numpy as jnp
from jax import lax
from jax.experimental import pallas as pl
from jax.experimental.pallas import tpu as pltpu
from jax.sharding import PartitionSpec as P

CAP = 10
ROWS = 16
SPARE = ROWS - CAP
LANES = 128
TAIL = 4 * LANES
BF = jnp.bfloat16
F32 = jnp.float32
MESH = pl.DeviceIdType.MESH
NT = ((1,), (1,))


def dot(a, b, dims=((1,), (0,)), precision=None):
    return lax.dot_general(
        a, b, (dims, ((), ())), preferred_element_type=F32, precision=precision
    )


def iota(shape, dim):
    return lax.broadcasted_iota(jnp.int32, shape, dim)


def hot(condition):
    return jnp.where(condition, 1.0, 0.0).astype(BF)


def hops(nz):
    near = [1, 2] if nz > 8 else []
    pairs = []
    for d in range(nz // 2 - 1, len(near), -1):
        pairs += [d] + near[len(pairs) // 2 : len(pairs) // 2 + 1]
    return [nz // 2] + [d for pair in pairs for d in (pair, nz - pair)]


def kernel(
    nz, ny,
    tok, cot, ids_ref, probs_ref, wg, wu, wd,
    tg_ref, pg_ref, gg_ref, gu_ref, gd_ref,
    w, tq, cq, sb, rb, xs, ds, mx, md, gt, mgt, ch, cs, yl, yr, ip, xq, pk, rs, rr,
    ld, zs, zr, fs, fr, ms, mr, ps, pr, hs, hr, ys, yrs, vs, vr,
):
    t, z, island = lax.axis_index("tp"), lax.axis_index("ep"), lax.axis_index("island")
    y = lax.div(island, 2)
    core = island - 2 * y
    toks, quarter = tq.shape
    ff = wg.shape[0]
    m = nz * CAP
    n = nz * ROWS
    half = m // 2
    band = xs.shape[3]
    pairs = xs.shape[0]
    hz, hy = nz // 2, ny // 2
    piece_rows = 3 * ff // 4

    def tp_at(r):
        return {"tp": lax.rem(t + r, 4)}

    def ep_at(d):
        return {"ep": lax.rem(z + d, nz)}

    def y_at(d):
        return {"island": 2 * lax.rem(y + d, ny) + core}

    mate = {"island": 2 * y + 1 - core}

    def remote(src, dst, ssem, rsem, device):
        return pltpu.make_async_remote_copy(
            src_ref=src, dst_ref=dst, send_sem=ssem, recv_sem=rsem,
            device_id=device, device_id_type=MESH,
        )

    loads = [
        pltpu.make_async_copy(tok.at[:, pl.ds(pl.multiple_of(t * quarter, quarter), quarter)], tq, ld.at[0]),
        pltpu.make_async_copy(cot.at[:, pl.ds(pl.multiple_of(t * quarter, quarter), quarter)], cq, ld.at[1]),
        pltpu.make_async_copy(wg, w.at[pl.ds(0, ff)], ld.at[2]),
        pltpu.make_async_copy(wu, w.at[pl.ds(ff, ff)], ld.at[3]),
        pltpu.make_async_copy(wd, w.at[pl.ds(2 * ff, ff)], ld.at[4]),
    ]
    for copy in loads:
        copy.start()

    barrier = pltpu.get_barrier_semaphore()
    peers = [ep_at(d) for d in range(1, nz)] + [tp_at(r) for r in (1, 2, 3)]
    peers += [y_at(1), y_at(ny - 1), mate]
    for peer in peers:
        pl.semaphore_signal(barrier, inc=1, device_id=peer, device_id_type=MESH)

    ids = ids_ref[...]
    probs = probs_ref[...]
    named = hot(iota((nz, toks), 0) == ids)
    earlier = hot(iota((toks, toks), 0) < iota((toks, toks), 1))
    rank = jnp.sum(named.astype(F32) * dot(named, earlier), 0, keepdims=True)
    eye = iota((toks, toks), 0) == iota((toks, toks), 1)

    def column(row):
        return jnp.sum(jnp.where(eye, row, 0.0), 1, keepdims=True)

    probs_col = column(probs)
    ids_col = column(ids.astype(F32)).astype(jnp.int32)
    rank_col = column(rank).astype(jnp.int32)
    rank = rank.astype(jnp.int32)

    place = iota((n, toks), 0)
    block, row = lax.shift_right_logical(place, 4), place & (ROWS - 1)
    mine = block == ids
    pick_x = hot(mine & (row == rank))
    pick_d = hot(mine & (row == rank + CAP))
    piece = lax.shift_right_logical(row, 2)
    late = mine & ((row & 3) + SPARE == rank)
    pick_tail = [hot(late & (piece == c)) for c in range(4)]

    loads[0].wait()
    loads[1].wait()
    own_x = tq[...]
    own_d = (cq[...].astype(F32) * probs_col).astype(BF)
    main = dot(jnp.concatenate([pick_x, pick_d], 1), jnp.concatenate([own_x, own_d], 0))
    tail = dot(
        jnp.concatenate(pick_tail, 1),
        jnp.concatenate([own_d[:, LANES * c : LANES * (c + 1)] for c in range(4)], 0),
    )
    sb[:, :, 0:quarter] = main.astype(BF).reshape(nz, ROWS, quarter)
    sb[:, :, quarter : quarter + LANES] = tail.astype(BF).reshape(nz, ROWS, LANES)

    pl.semaphore_wait(barrier, len(peers))

    order = hops(nz)

    def z_copy(k):
        d = order[k]
        return remote(sb.at[lax.rem(z + d, nz)], rb.at[t, k + 1], zs.at[k], zr.at[k], ep_at(d))

    z_copies = [z_copy(k) for k in range(nz - 1)]
    own_block = pltpu.make_async_copy(sb.at[z], rb.at[t, 0], ld.at[5])
    own_block.start()
    for copy in z_copies:
        copy.start()

    left_q, right_q, far_q = lax.rem(t + 3, 4), lax.rem(t + 1, 4), lax.rem(t + 2, 4)

    def pass_right(p):
        return remote(rb.at[t, p], rb.at[t, p], fs.at[0, p], fr.at[0, p], tp_at(1))

    def pass_left(p):
        return remote(rb.at[t, p], rb.at[t, p], fs.at[1, p], fr.at[1, p], tp_at(3))

    def from_left(p):
        return remote(rb.at[t, p], rb.at[left_q, p], fs.at[0, p], fr.at[0, p], tp_at(1))

    def from_right(p):
        return remote(rb.at[t, p], rb.at[right_q, p], fs.at[1, p], fr.at[1, p], tp_at(3))

    direct = nz - 4 if nz > 8 else nz // 2

    def onward(p):
        if p >= direct:
            return remote(rb.at[t, p], rb.at[t, p], fs.at[2, p], fr.at[2, p], tp_at(2))
        q, to = (right_q, 3) if p % 2 else (left_q, 1)
        return remote(rb.at[q, p], rb.at[q, p], fs.at[2, p], fr.at[2, p], tp_at(to))

    def from_far(p):
        return remote(rb.at[t, p], rb.at[far_q, p], fs.at[2, p], fr.at[2, p], tp_at(1))

    def relay(p):
        from_left(p).wait_recv()
        from_right(p).wait_recv()
        onward(p).start()

    behind = 2
    for p in range(nz):
        if p == 0:
            own_block.wait()
        else:
            z_copies[p - 1].wait_recv()
        if p >= direct:
            onward(p).start()
        pass_right(p).start()
        pass_left(p).start()
        if 0 <= p - behind < direct:
            relay(p - behind)
    for p in range(max(0, nz - behind), direct):
        relay(p)

    rows = iota((half, n // 2), 0)
    source = lax.shift_right_logical(rows * 6554, 16)
    slot = rows - CAP * source
    there = iota((half, n // 2), 1)
    unpick_x = hot(there == ROWS * source + slot)
    unpick_d = hot((slot < SPARE) & (there == ROWS * source + CAP + slot))
    unpick_tail = [
        hot((slot >= SPARE) & (there == ROWS * source + 4 * c + slot - SPARE)) for c in range(4)
    ]
    unpick_main = jnp.concatenate([unpick_x, unpick_d], 0)
    unpick_tail = jnp.concatenate(unpick_tail, 0)
    per = quarter // band
    for g in range(2):
        for p in range(g * hz, g * hz + hz):
            if p >= direct:
                from_left(p).wait_recv()
                from_right(p).wait_recv()
            from_far(p).wait_recv()
        here = pl.ds(g * half, half)
        for q in range(4):
            got = rb[q, pl.ds(g * hz, hz)].reshape(n // 2, quarter + LANES)
            both = dot(unpick_main, got[:, 0:quarter])
            ends = dot(unpick_tail, got[:, quarter : quarter + LANES])
            ends = jnp.concatenate([ends[half * c : half * (c + 1)] for c in range(4)], 1)
            x_rows = both[0:half].astype(BF)
            d_rows = (both[half : 2 * half] + ends).astype(BF)
            for b in range(per):
                at = q * per + b
                xs[at // 2, at % 2, here, :] = x_rows[:, band * b : band * (b + 1)]
                ds[at // 2, at % 2, here, :] = d_rows[:, band * b : band * (b + 1)]

    mate_x = remote(xs.at[:, 1 - core], mx, ms.at[0], mr.at[0], mate)
    mate_d = remote(ds.at[:, 1 - core], md, ms.at[1], mr.at[1], mate)
    mate_g = remote(gt, mgt, ms.at[2], mr.at[2], mate)
    mate_x.start()
    mate_d.start()

    for copy in loads[2:]:
        copy.wait()
    x_all = jnp.concatenate([xs[o, c] for o in range(pairs) for c in range(2)], 1)
    d_all = jnp.concatenate([ds[o, c] for o in range(pairs) for c in range(2)], 1)
    gate_up = dot(w[0 : 2 * ff, :], x_all, NT)
    back = dot(w[2 * ff : 3 * ff, :], d_all, NT)
    gate, up = gate_up[0:ff], gate_up[ff : 2 * ff]
    sigma = jax.nn.sigmoid(gate)
    active = gate * sigma
    hidden = (active * up).astype(BF)
    gt[0:ff, :] = (back * up * sigma * (1.0 + gate * (1.0 - sigma))).astype(BF)
    gt[ff : 2 * ff, :] = (back * active).astype(BF)
    gt[2 * ff : 3 * ff, :] = hidden
    mate_g.start()

    eye_m = hot(iota((m, m), 0) == iota((m, m), 1))
    d_rows = dot(eye_m, gt[0 : 2 * ff, :], NT).astype(BF)

    def input_part(r):
        q = lax.rem(t + r, 4)
        cols = pl.ds(pl.multiple_of(q * quarter, quarter), quarter)
        ip[r] = dot(d_rows, w[0 : 2 * ff, cols]).astype(BF)

    def tp_copy(g, r):
        here = pl.ds(g * half, half)
        return remote(ip.at[r, here], xq.at[r - 1, here], hs.at[g, r], hr.at[g, r], tp_at(r))

    tp_copies = [[tp_copy(g, r) for r in (1, 2, 3)] for g in range(2)]

    def weight_part(*js):
        def cat(blocks):
            return blocks[0] if len(blocks) == 1 else jnp.concatenate(blocks, 1)

        os = [lax.rem(y + j, ny) for j in js]
        top = dot(gt[0 : 2 * ff, :], cat([xs[o, core] for o in os]))
        top = top + dot(mgt[0 : 2 * ff, :], cat([mx[o] for o in os]))
        low = dot(gt[2 * ff : 3 * ff, :], cat([ds[o, core] for o in os]))
        low = low + dot(mgt[2 * ff : 3 * ff, :], cat([md[o] for o in os]))
        for i, j in enumerate(js):
            ch[j, 0 : 2 * ff, :] = top[:, band * i : band * (i + 1)]
            ch[j, 2 * ff : 3 * ff, :] = low[:, band * i : band * (i + 1)]

    def y_copy(side, dist, part):
        j = dist if side == 0 else ny - dist
        where = pl.ds(part * piece_rows, piece_rows)
        into = (yl, yr)[side]
        return remote(
            cs.at[j, where], into.at[dist - 1, where],
            ys.at[side, dist, part], yrs.at[side, dist, part], y_at(1 if side == 0 else ny - 1),
        )

    far_parts, near_parts = ((0, 1), (2, 3)), ((2, 3), (0, 1))

    def y_step(side, dist, part):
        j = dist if side == 0 else ny - dist
        where = pl.ds(part * piece_rows, piece_rows)
        if dist == hy or (dist == hy - 1 and part in near_parts[side]):
            cs[j, where, :] = ch[j, where, :].astype(BF)
        else:
            y_copy(side, dist + 1, part).wait_recv()
            came = (yl, yr)[side][dist, where, :].astype(F32)
            cs[j, where, :] = (ch[j, where, :] + came).astype(BF)
        y_copy(side, dist, part).start()

    def y_steps(dist, parts):
        for i in range(2):
            for side in (0, 1):
                y_step(side, dist, parts[side][i])

    for r in (2, 1, 3):
        input_part(r)
        tp_copies[0][r - 1].start()
    for r in (2, 1, 3):
        tp_copies[1][r - 1].start()

    mate_x.wait_recv()
    mate_d.wait_recv()
    mate_g.wait_recv()
    weight_part(hy)
    y_steps(hy, far_parts)
    weight_part(hy - 1, ny - hy + 1)
    y_steps(hy - 1, near_parts)

    prob_row = jnp.sum(hidden.astype(F32) * back, 0, keepdims=True)
    in_source = iota((nz, m), 0) == lax.shift_right_logical(iota((nz, m), 1) * 6554, 16)
    at_row = iota((m, LANES), 0)
    at_slot = iota((m, LANES), 1) == at_row - CAP * lax.shift_right_logical(at_row * 6554, 16)
    pk[0] = dot(
        jnp.where(in_source, prob_row, 0.0), jnp.where(at_slot, 1.0, 0.0),
        precision=lax.Precision.HIGHEST,
    )
    prob_sends = [remote(pk.at[0], pk.at[r], ps.at[r], pr.at[r], tp_at(r)) for r in (1, 2, 3)]
    for copy in prob_sends:
        copy.start()
    input_part(0)
    y_steps(hy - 1, far_parts)
    for copy in prob_sends:
        copy.wait_recv()
    prob = (pk[0] + pk[1]) + (pk[2] + pk[3])
    prob_high = prob.astype(BF)
    prob_low = (prob - prob_high.astype(F32)).astype(BF)
    to = iota((n // 2, half), 0)
    block, row = lax.shift_right_logical(to, 4), to & (ROWS - 1)
    first = CAP * block
    frm = iota((n // 2, half), 1)
    pack = hot((row < CAP) & (frm == first + row))
    pack_0 = hot((row >= CAP) & (frm == first + row - CAP))
    pack_1 = hot((row >= CAP) & (row < ROWS - 2) & (frm == first + row - CAP + SPARE))
    to = iota((n // 2, nz), 0)
    block, row = lax.shift_right_logical(to, 4), to & (ROWS - 1)

    def back_copy(k):
        d = nz - order[k]
        return remote(rs.at[k + 1], rr.at[z], vs.at[k], vr.at[k], ep_at(d))

    def back_recv(k):
        return remote(rs.at[0], rr.at[lax.rem(z + order[k], nz)], vs.at[k], vr.at[k], ep_at(1))

    def send_back(g):
        for copy in tp_copies[g]:
            copy.wait_recv()
        here = pl.ds(g * half, half)
        summed = ip[0, here, :].astype(F32) + xq[0, here, :].astype(F32)
        summed = summed + (xq[1, here, :].astype(F32) + xq[2, here, :].astype(F32))
        summed = summed.astype(BF)
        ends = summed[:, 3 * LANES : 4 * LANES]
        same = block + g * hz == iota((n // 2, nz), 1)
        extra = dot(hot(same & (row == CAP)), prob_high) + dot(hot(same & (row == CAP + 1)), prob_low)
        packed = dot(pack, summed[:, 0 : 3 * LANES])
        packed = packed + jnp.concatenate([dot(pack_0, ends), dot(pack_1, ends), extra], 1)
        rs[pl.ds(g * hz, hz)] = packed.astype(BF).reshape(hz, ROWS, 3 * LANES)
        for k in range(max(g * hz - 1, 0), g * hz + hz - 1):
            back_copy(k).start()

    send_back(0)
    if hy > 2:
        weight_part(hy - 2, ny - hy + 2)
        y_steps(hy - 2, near_parts)
    send_back(1)
    own_back = pltpu.make_async_copy(rs.at[0], rr.at[z], ld.at[6])
    own_back.start()
    for dist in range(hy - 2, 0, -1):
        if dist < hy - 2:
            y_steps(dist, near_parts)
        else:
            for at in range(dist - 1, 0, -1):
                weight_part(at, ny - at)
        y_steps(dist, far_parts)
    weight_part(0)

    for copy in z_copies + [mate_x, mate_d, mate_g] + prob_sends + tp_copies[0] + tp_copies[1]:
        copy.wait_send()
    for p in range(nz):
        pass_right(p).wait_send()
        pass_left(p).wait_send()
        onward(p).wait_send()
    for side in (0, 1):
        for dist in range(hy, 1, -1):
            for part in range(4):
                if dist < hy or part in far_parts[side]:
                    y_copy(side, dist, part).wait_send()
    for parts_at in (near_parts, far_parts):
        for i in range(2):
            for side in (0, 1):
                y_copy(side, 1, parts_at[side][i]).wait_recv()
    total = ch[0] + (yl[0].astype(F32) + yr[0].astype(F32))
    gg_ref[...] = total[0:ff]
    gu_ref[...] = total[ff : 2 * ff]
    gd_ref[...] = total[2 * ff : 3 * ff]

    at = iota((toks, n), 1)
    block, row = lax.shift_right_logical(at, 4), at & (ROWS - 1)
    mine = block == ids_col
    take = hot(mine & (row == rank_col))
    take_0 = hot(mine & (row == rank_col + CAP) & (rank_col < SPARE))
    take_1 = hot(mine & (row == rank_col + CAP - SPARE) & (rank_col >= SPARE))
    take_high, take_low = hot(mine & (row == CAP)), hot(mine & (row == CAP + 1))

    for k in range(nz - 1):
        back_recv(k).wait_recv()
    own_back.wait()
    got = rr[...].reshape(n, 3 * LANES)
    tg_ref[:, 0 : 3 * LANES] = dot(take, got).astype(BF)
    tg_ref[:, 3 * LANES : 4 * LANES] = (
        dot(take_0, got[:, 0:LANES]) + dot(take_1, got[:, LANES : 2 * LANES])
    ).astype(BF)
    ends = got[:, 2 * LANES : 3 * LANES]
    chosen = iota((toks, LANES), 1) == rank_col
    value = jnp.where(chosen, dot(take_high, ends) + dot(take_low, ends), 0.0)
    value = jnp.sum(value, 1, keepdims=True) / probs_col
    pg_ref[...] = jnp.sum(jnp.where(eye, value, 0.0), 0, keepdims=True)

    for k in range(nz - 1):
        back_copy(k).wait_send()
    for side in (0, 1):
        for part in range(4):
            if hy > 1 or part in far_parts[side]:
                y_copy(side, 1, part).wait_send()


def publish(*refs):
    copies = [pltpu.make_async_copy(refs[i], refs[i + 5], refs[10].at[i]) for i in range(5)]
    for copy in copies:
        copy.start()
    for copy in copies:
        copy.wait()


def shards(tokens, cotangent, expert_ids, gate_probs, w_gate, w_up, w_down):
    toks, width = tokens.shape
    ff = w_down.shape[1]
    nz, ny = lax.axis_size("ep"), lax.axis_size("island") // 2
    quarter, band = width // 4, width // (2 * ny)
    m = nz * CAP
    wide = quarter + LANES
    hy, hz = ny // 2, nz // 2
    hbm = pl.BlockSpec(memory_space=pltpu.HBM)
    vmem = pl.BlockSpec(memory_space=pltpu.VMEM)
    dma = pltpu.SemaphoreType.DMA
    shapes = (
        jax.ShapeDtypeStruct((toks, quarter), BF),
        jax.ShapeDtypeStruct((1, toks), F32),
        jax.ShapeDtypeStruct((ff, band), F32),
        jax.ShapeDtypeStruct((ff, band), F32),
        jax.ShapeDtypeStruct((ff, band), F32),
    )
    results = pl.pallas_call(
        functools.partial(kernel, nz, ny),
        out_shape=shapes,
        in_specs=[hbm, hbm, vmem, vmem, hbm, hbm, hbm],
        out_specs=(vmem,) * 5,
        scratch_shapes=[
            pltpu.VMEM((3 * ff, width), BF),
            pltpu.VMEM((toks, quarter), BF),
            pltpu.VMEM((toks, quarter), BF),
            pltpu.VMEM((nz, ROWS, wide), BF),
            pltpu.VMEM((4, nz, ROWS, wide), BF),
            pltpu.VMEM((ny, 2, m, band), BF),
            pltpu.VMEM((ny, 2, m, band), BF),
            pltpu.VMEM((ny, m, band), BF),
            pltpu.VMEM((ny, m, band), BF),
            pltpu.VMEM((3 * ff, m), BF),
            pltpu.VMEM((3 * ff, m), BF),
            pltpu.VMEM((ny, 3 * ff, band), F32),
            pltpu.VMEM((ny, 3 * ff, band), BF),
            pltpu.VMEM((hy, 3 * ff, band), BF),
            pltpu.VMEM((hy, 3 * ff, band), BF),
            pltpu.VMEM((4, m, quarter), BF),
            pltpu.VMEM((3, m, quarter), BF),
            pltpu.VMEM((4, nz, LANES), F32),
            pltpu.VMEM((nz, ROWS, 3 * LANES), BF),
            pltpu.VMEM((nz, ROWS, 3 * LANES), BF),
            dma((7,)),
            dma((nz,)), dma((nz,)),
            dma((3, nz)), dma((3, nz)),
            dma((3,)), dma((3,)),
            dma((4,)), dma((4,)),
            dma((2, 4)), dma((2, 4)),
            dma((2, hy + 1, 4)), dma((2, hy + 1, 4)),
            dma((nz,)), dma((nz,)),
        ],
        compiler_params=pltpu.CompilerParams(
            collective_id=0, has_side_effects=True, vmem_limit_bytes=(53 * 1024 + 384) * 1024
        ),
    )(
        tokens, cotangent,
        expert_ids.reshape(1, toks), gate_probs.reshape(1, toks),
        w_gate[0].T, w_up[0].T, w_down[0],
    )
    anywhere = pl.BlockSpec(memory_space=pl.ANY)
    token_grad, prob_grad, grad_gate, grad_up, grad_down = pl.pallas_call(
        publish,
        out_shape=shapes,
        in_specs=[anywhere] * 5,
        out_specs=(anywhere,) * 5,
        scratch_shapes=[dma((5,))],
        compiler_params=pltpu.CompilerParams(vmem_limit_bytes=4 * 1024 * 1024),
    )(*results)
    return (
        token_grad, prob_grad.reshape(toks, 1),
        grad_gate.T[None], grad_up.T[None], grad_down[None],
    )


def solution(mesh):
    rows = P(("island", "ep"), None)
    in_specs = (rows, rows, rows, rows, P("ep", None, "tp"), P("ep", None, "tp"), P("ep", "tp", None))
    out_specs = (
        P(("island", "ep"), "tp"), rows,
        P("ep", "island", "tp"), P("ep", "island", "tp"), P("ep", "tp", "island"),
    )
    return jax.shard_map(shards, mesh=mesh, in_specs=in_specs, out_specs=out_specs, check_vma=False)
```
